32 devices in a mesh: nodes: 16 (over z, y, x), heads: 2 (over core).
Axes of the slice: x: 2, y: 2, z: 4, core: 2. Of those that a mesh axis runs over, the one named last changes fastest.
Arguments:
- inputs: bfloat16 [14336, 512], P('nodes', 'heads'), may hold values from -6 to 6
- w_query: bfloat16 [512, 512], P(None, 'heads'), may hold values from -0.375 to 0.375
- w_key: bfloat16 [512, 512], P(None, 'heads'), may hold values from -0.375 to 0.375
- w_value: bfloat16 [512, 512], P(None, 'heads'), may hold values from -0.25 to 0.25
- w_out: bfloat16 [512, 512], P('heads'), may hold values from -1 to 1
- w_up: bfloat16 [512, 2048], P(None, 'heads'), may hold values from -0.25 to 0.25
- w_down: bfloat16 [2048, 512], P('heads'), may hold values from -0.125 to 0.125
- mod_table: float32 [4, 16, 512], replicated, may hold values from -2.5 to 2.5
- level_ids: int32 [14336], P('nodes'), may hold values from 0 to 15
- neighbours: int32 [14336, 16], P('nodes'), may hold values from 0 to 14335, as said below
- cotangent: bfloat16 [14336, 512], P('nodes', 'heads'), may hold values from -6 to 6
Outputs:
- output: bfloat16 [14336, 512], P('nodes', 'heads')
- grad_inputs: float32 [14336, 512], P('nodes', 'heads')
- grad_query: float32 [512, 512], P(None, 'heads')
- grad_key: float32 [512, 512], P(None, 'heads')
- grad_value: float32 [512, 512], P(None, 'heads')
- grad_out: float32 [512, 512], P('heads')
- grad_up: float32 [512, 2048], P(None, 'heads')
- grad_down: float32 [2048, 512], P('heads')
- grad_table: float32 [4, 16, 512], P(None, None, 'heads')
The draws below stay inside these ranges and needn't reach their ends.
Inputs may be any that keep to these rules, and one draw needn't show every extreme that they name: `neighbours`: each row holds 16 distinct node indices, none equal to the row's own node, each within 896 of it in the cyclic order of all 14336 nodes.
All inputs are finite; a program needn't handle non-finite values.
Results may differ from the reference program's by a relative error of at most 0.015.
Values may be sent and summed in bfloat16 or wider, within the bound.
No kernel may reach another device: no remote copies, remote signals or barrier semaphores. Data moves between devices by JAX's collectives and lax.ppermute only.
A program may use at most 128 MiB of HBM per device.

```python
import math
import jax
import jax.numpy as jnp
from jax import lax

D = 512
HEADS = 4
HD = 128
FF = 2048
K = 16
LEVELS = 16
NODES = 14336
SPAN = 896


def draw_neighbours(key, part):
    key = jax.random.fold_in(key, 7)
    stratum = 2 * SPAN // K
    chosen = jax.random.randint(key, (NODES, K), 0, stratum)
    candidate = jnp.arange(K, dtype=jnp.int32)[None, :] * stratum + chosen
    offset = jnp.where(candidate < SPAN, candidate - SPAN, candidate - SPAN + 1)
    nodes_here = jnp.arange(NODES, dtype=jnp.int32)[:, None]
    return jnp.mod(nodes_here + offset, NODES).astype(jnp.int32)


def with_ends(result, own_key, low, high):
    longest = result.shape.index(max(result.shape))
    spots = []
    for shift in (0, 1):
        where = [jax.random.randint(jax.random.fold_in(own_key, axis), (), 0, length) for axis, length in enumerate(result.shape)]
        where[longest] = (where[longest] + shift) % result.shape[longest]
        spots.append(tuple(where))
    return result.at[spots[0]].set(low).at[spots[1]].set(high)


def level_of(stream_key, dims, pieces, smallest, top_value):
    level = 1.0
    for axis_at, shards_of in pieces:
        steps = jax.random.uniform(jax.random.fold_in(jax.random.fold_in(stream_key, 6), axis_at), (shards_of,), jnp.float32, smallest / len(pieces), top_value / len(pieces))
        level = level * jnp.repeat(jnp.exp(steps), dims[axis_at] // shards_of).reshape((-1,) + (1,) * (len(dims) - 1 - axis_at))
    return level


def bell_draw(stream_key, shape, spread, reach, pieces=(), held_as=jnp.bfloat16):
    values = spread * jax.random.normal(stream_key, shape, jnp.float32)
    if pieces:
        values = values * level_of(stream_key, shape, pieces, -0.22, 0.18)
    return jnp.clip(values, -reach, reach).astype(held_as)


def setup_inputs(seed: int = 0) -> dict:
    arg_keys = jax.random.split(jax.random.key(seed), 12)
    return {
        "inputs": bell_draw(arg_keys[0], (NODES, D), 1.0, 6.0, ((0, 16), (1, 2))),
        "w_query": bell_draw(arg_keys[1], (D, HEADS * HD), (D // 2) ** -0.5, 0.375, ((1, 2),)),
        "w_key": bell_draw(arg_keys[2], (D, HEADS * HD), (D // 2) ** -0.5, 0.375, ((1, 2),)),
        "w_value": bell_draw(arg_keys[3], (D, HEADS * HD), D ** -0.5, 0.25, ((1, 2),)),
        "w_out": bell_draw(arg_keys[4], (HEADS * HD, D), (HEADS * HD // K) ** -0.5, 1.0, ((0, 2),)),
        "w_up": bell_draw(arg_keys[5], (D, FF), D ** -0.5, 0.25, ((1, 2),)),
        "w_down": bell_draw(arg_keys[6], (FF, D), FF ** -0.5, 0.125, ((0, 2),)),
        "mod_table": bell_draw(arg_keys[7], (4, LEVELS, D), 0.3, 2.5, (), jnp.float32),
        "level_ids": with_ends(jax.random.randint(arg_keys[8], (NODES,), 0, LEVELS), jax.random.fold_in(arg_keys[8], 1), 0, LEVELS - 1).astype(jnp.int32),
        "neighbours": draw_neighbours(jax.random.fold_in(arg_keys[11], 71), 0),
        "cotangent": bell_draw(arg_keys[10], (NODES, D), 1.0, 6.0, ((0, 16), (1, 2))),
    }


epsilon = 1e-05
highest = lax.Precision.HIGHEST

@jax.custom_vjp
def low(v):
    return lax.optimization_barrier(v.astype(jnp.bfloat16)).astype(jnp.float32)

@jax.custom_vjp
def low_back(v):
    return v

def low_keep(v):
    return (low(v), None)

def low_pass(kept, grad):
    return (grad,)

def back_keep(v):
    return (v, None)

def back_low(kept, grad):
    return (low(grad),)
low.defvjp(low_keep, low_pass)
low_back.defvjp(back_keep, back_low)

def product(left, right):
    return jnp.dot(left, right, precision=highest)

def norm_rows(values):
    row_mean = lax.optimization_barrier(jnp.mean(values, axis=1, keepdims=True))
    centred = values - row_mean
    variance = lax.optimization_barrier(jnp.mean(centred * centred, axis=1, keepdims=True))
    return centred * lax.rsqrt(variance + epsilon)

def layer(inputs, w_query, w_key, w_value, w_out, w_up, w_down, mod_table, onehot, neighbours):
    scale_a = product(onehot, mod_table[0])
    shift_a = product(onehot, mod_table[1])
    scale_b = product(onehot, mod_table[2])
    shift_b = product(onehot, mod_table[3])
    normed_one = low(norm_rows(inputs) * (1.0 + scale_a) + shift_a)
    queries = low_back(low(product(normed_one, w_query)))
    keys = low_back(low(product(normed_one, w_key)))
    values = low_back(low(product(normed_one, w_value)))
    block_rows = math.gcd(NODES, 4096)
    block_count = NODES // block_rows
    query_blocks = queries.reshape(block_count, block_rows, HEADS, HD)
    index_blocks = neighbours.reshape(block_count, block_rows, K)

    def attend(operands):
        query_block, index_block = operands
        key_block = keys[index_block].reshape(block_rows, K, HEADS, HD)
        value_block = values[index_block].reshape(block_rows, K, HEADS, HD)
        scores = jnp.einsum('bhd,bkhd->bkh', query_block, key_block, precision=highest) / math.sqrt(HD)
        probs = jax.nn.softmax(scores, axis=1)
        return jnp.einsum('bkh,bkhd->bhd', probs, value_block, precision=highest)
    mixed = lax.map(jax.checkpoint(attend), (query_blocks, index_blocks)).reshape(NODES, HEADS * HD)
    middle = inputs + low_back(product(low(mixed), w_out))
    normed_two = low(norm_rows(middle) * (1.0 + scale_b) + shift_b)
    pre_act = low_back(product(normed_two, w_up))
    activated = low(jax.nn.silu(pre_act))
    return middle + product(activated, w_down)

def reference(inputs, w_query, w_key, w_value, w_out, w_up, w_down, mod_table, level_ids, neighbours, cotangent):
    onehot = (level_ids[:, None] == jnp.arange(LEVELS, dtype=jnp.int32)[None, :]).astype(jnp.float32)
    floats = [weight.astype(jnp.float32) for weight in (inputs, w_query, w_key, w_value, w_out, w_up, w_down, mod_table)]

    def forward(*operands):
        return layer(*operands, onehot, neighbours)
    output, pullback = jax.vjp(forward, *floats)
    gradients = pullback(cotangent.astype(jnp.float32))
    return (output.astype(jnp.bfloat16), gradients[0], gradients[1], gradients[2], gradients[3], gradients[4], gradients[5], gradients[6], gradients[7])
```

```python
import math

import jax
import jax.numpy as jnp
from jax import lax
from jax.experimental import pallas as pl
from jax.experimental.pallas import tpu as pltpu
from jax.sharding import PartitionSpec as P

HD = 128
K = 16
SPAN = 896
ROWS = 128
WORD = 64
epsilon = 1e-05
highest = lax.Precision.HIGHEST
HUGE = -1e30
VMEM = 56 * 1024 * 1024


def dot(left, right, left_dim, right_dim):
    return lax.dot_general(
        left,
        right,
        (((left_dim,), (right_dim,)), ((), ())),
        preferred_element_type=jnp.float32,
    )


def two_blocks(first, second):
    zero = jnp.zeros_like(first)
    return jnp.concatenate(
        [jnp.concatenate([first, zero], 1), jnp.concatenate([zero, second], 1)], 0
    )


def forward_kernel(nbr_ref, q_ref, k_ref, vt_ref, e_ref, mixed_ref, inv_ref):
    block = pl.program_id(0)
    start = pl.multiple_of(block * ROWS, ROWS)
    window = e_ref.shape[1]
    factor = 1.0 / math.sqrt(HD)
    scale = factor * math.log2(math.e)
    place = nbr_ref[:, pl.ds(start, ROWS)] - start
    bit = jnp.left_shift(1, jnp.right_shift(place, 6))
    low = jnp.bitwise_and(place, WORD - 1)
    lane_low = lax.broadcasted_iota(jnp.int32, (WORD, ROWS), 0)
    words = jnp.zeros((WORD, ROWS), jnp.int32)
    for j in range(K):
        words = words | jnp.where(lane_low == low[j : j + 1, :], bit[j : j + 1, :], 0)
    words = jnp.concatenate([words, words], 1)
    queries = q_ref[pl.ds(start, ROWS), :]
    both = two_blocks(queries[:, :HD], queries[:, HD:])
    scores = dot(k_ref[pl.ds(start, window), :], both, 1, 1)
    masked = []
    for t in range(window // WORD):
        keep = (words & (1 << t)) != 0
        masked.append(jnp.where(keep, scores[t * WORD : (t + 1) * WORD, :], HUGE))
    top = masked[0]
    for part in masked[1:]:
        top = jnp.maximum(top, part)
    top = jnp.max(top, axis=0, keepdims=True) * scale
    total = jnp.zeros((WORD, 2 * ROWS), jnp.float32)
    weights = []
    for part in masked:
        weight = jnp.exp2(part * scale - top)
        total = total + weight
        weights.append(weight.astype(jnp.bfloat16))
    inverse = 1.0 / jnp.sum(total, axis=0, keepdims=True)
    weights = jnp.concatenate(weights, 0)
    e_ref[0] = weights
    inv_ref[0] = jnp.broadcast_to(inverse, inv_ref.shape[1:])
    mixed = dot(vt_ref[:, pl.ds(start, window)], weights, 1, 0) * inverse
    mixed_ref[:, :HD] = mixed[:HD, :ROWS].T.astype(jnp.bfloat16)
    mixed_ref[:, HD:] = mixed[HD:, ROWS:].T.astype(jnp.bfloat16)


def attend(places, queries, keys, values_t):
    rows = queries.shape[0]
    wide = 2 * HD
    blocks = rows // ROWS
    window = ROWS + 2 * SPAN
    return pl.pallas_call(
        forward_kernel,
        grid=(blocks,),
        in_specs=[
            pl.BlockSpec(places.shape, lambda b: (0, 0)),
            pl.BlockSpec(queries.shape, lambda b: (0, 0)),
            pl.BlockSpec(keys.shape, lambda b: (0, 0)),
            pl.BlockSpec(values_t.shape, lambda b: (0, 0)),
        ],
        out_specs=[
            pl.BlockSpec((1, window, wide), lambda b: (b, 0, 0)),
            pl.BlockSpec((ROWS, wide), lambda b: (b, 0)),
            pl.BlockSpec((1, 8, wide), lambda b: (b, 0, 0)),
        ],
        out_shape=[
            jax.ShapeDtypeStruct((blocks, window, wide), jnp.bfloat16),
            jax.ShapeDtypeStruct((rows, wide), jnp.bfloat16),
            jax.ShapeDtypeStruct((blocks, 8, wide), jnp.float32),
        ],
        compiler_params=pltpu.CompilerParams(vmem_limit_bytes=VMEM),
        name="attend_forward",
    )(places, queries, keys, values_t)


def backward_kernel(
    e_ref, inv_ref, q_ref, kt_ref, v_ref, gt_ref, dq_ref, dk_ref, dv_ref, dk_sum, dv_sum
):
    block = pl.program_id(0)
    start = pl.multiple_of(block * ROWS, ROWS)
    window = e_ref.shape[1]
    factor = 1.0 / math.sqrt(HD)

    @pl.when(block == 0)
    def _():
        dk_sum[...] = jnp.zeros_like(dk_sum)
        dv_sum[...] = jnp.zeros_like(dv_sum)

    inverse = inv_ref[0][:1, :]
    queries = q_ref[pl.ds(start, ROWS), :]
    both = two_blocks(queries[:, :HD], queries[:, HD:])
    grad = gt_ref[:, pl.ds(start, ROWS)]
    grad_both = two_blocks(
        (grad[:HD, :] * inverse[:, :ROWS]).astype(jnp.bfloat16),
        (grad[HD:, :] * inverse[:, ROWS:]).astype(jnp.bfloat16),
    )
    weights = e_ref[0]
    spots = pl.ds(start, window)
    grad_probs = dot(v_ref[spots, :], grad_both, 1, 0)
    wide = weights.astype(jnp.float32)
    cross = jnp.sum(grad_probs * wide, axis=0, keepdims=True) * inverse
    grad_scores = (wide * (grad_probs - cross)).astype(jnp.bfloat16)
    dv_sum[spots, :] += dot(weights, grad_both, 1, 1)
    dk_sum[spots, :] += dot(grad_scores, both, 1, 0)
    grad_query = dot(kt_ref[:, spots], grad_scores, 1, 0) * factor
    dq_ref[:, :HD] = grad_query[:HD, :ROWS].T.astype(jnp.bfloat16)
    dq_ref[:, HD:] = grad_query[HD:, ROWS:].T.astype(jnp.bfloat16)

    @pl.when(block == pl.num_programs(0) - 1)
    def _():
        dk_ref[...] = (dk_sum[...] * factor).astype(dk_ref.dtype)
        dv_ref[...] = dv_sum[...].astype(dv_ref.dtype)


def attend_back(weights, inverse, queries, keys_t, values, grad_t):
    rows = queries.shape[0]
    wide = 2 * HD
    blocks, window, _ = weights.shape
    span_rows = values.shape[0]
    whole = lambda array: pl.BlockSpec(array.shape, lambda b: (0, 0))
    return pl.pallas_call(
        backward_kernel,
        grid=(blocks,),
        in_specs=[
            pl.BlockSpec((1, window, wide), lambda b: (b, 0, 0)),
            pl.BlockSpec((1, 8, wide), lambda b: (b, 0, 0)),
            whole(queries),
            whole(keys_t),
            whole(values),
            whole(grad_t),
        ],
        out_specs=[
            pl.BlockSpec((ROWS, wide), lambda b: (b, 0)),
            pl.BlockSpec((span_rows, wide), lambda b: (0, 0)),
            pl.BlockSpec((span_rows, wide), lambda b: (0, 0)),
        ],
        out_shape=[
            jax.ShapeDtypeStruct((rows, wide), jnp.bfloat16),
            jax.ShapeDtypeStruct((span_rows, wide), jnp.float32),
            jax.ShapeDtypeStruct((span_rows, wide), jnp.float32),
        ],
        scratch_shapes=[
            pltpu.VMEM((span_rows, wide), jnp.float32),
            pltpu.VMEM((span_rows, wide), jnp.float32),
        ],
        compiler_params=pltpu.CompilerParams(vmem_limit_bytes=VMEM),
        name="attend_backward",
    )(weights, inverse, queries, keys_t, values, grad_t)


def extended(block, sides, width):
    for axis, dim in sides:
        count = lax.axis_size(axis)
        forward = [(i, i + 1) for i in range(count - 1)]
        forward.append((count - 1, 0))
        backward = [(target, source) for source, target in forward]
        low = lax.ppermute(
            lax.slice_in_dim(block, block.shape[dim] - width, None, axis=dim), axis, forward
        )
        high = lax.ppermute(lax.slice_in_dim(block, 0, width, axis=dim), axis, backward)
        block = jnp.concatenate([low, block, high], axis=dim)
    return block


def passed_along(block, axis, distance):
    devices = range(lax.axis_size(axis))
    route = [((i - distance) % len(devices), i) for i in devices]
    return lax.ppermute(block, axis, route)


def contract_rows(left, right, precision=None):
    return lax.dot_general(
        left,
        right,
        (((0,), (0,)), ((), ())),
        precision=precision,
        preferred_element_type=jnp.float32,
    )


def contract_cols(left, right):
    return lax.dot_general(
        left, right, (((1,), (1,)), ((), ())), preferred_element_type=jnp.float32
    )


def norm_full(values):
    row_mean = jnp.mean(values, axis=1, keepdims=True)
    centred = values - row_mean
    variance = jnp.mean(centred * centred, axis=1, keepdims=True)
    inverse = lax.rsqrt(variance + epsilon)
    return (centred * inverse, inverse)


def body(
    inputs,
    w_query,
    w_key,
    w_value,
    w_out,
    w_up,
    w_down,
    mod_table,
    level_ids,
    neighbours,
    cotangent,
):
    node_rows = inputs.shape[0]
    half = inputs.shape[1]
    width = half * lax.axis_size("heads")
    local_width = w_query.shape[1]
    head_count = local_width // HD
    column_first = lax.axis_index("heads") * half
    factor = 1.0 / math.sqrt(HD)
    onehot = (
        level_ids[:, None] == jnp.arange(mod_table.shape[1], dtype=jnp.int32)[None, :]
    ).astype(jnp.float32)

    def level_rows(which):
        return jnp.dot(onehot, mod_table[which], precision=highest)

    full_in = lax.all_gather(inputs, "heads", axis=1, tiled=True).astype(jnp.float32)
    normed1, inverse1 = norm_full(full_in)
    normed_one = (normed1 * (1.0 + level_rows(0)) + level_rows(1)).astype(jnp.bfloat16)
    queries = jnp.dot(normed_one, w_query, preferred_element_type=jnp.float32).astype(jnp.bfloat16)
    keys = jnp.dot(normed_one, w_key, preferred_element_type=jnp.float32).astype(jnp.bfloat16)
    values = jnp.dot(normed_one, w_value, preferred_element_type=jnp.float32).astype(jnp.bfloat16)
    key_value = jnp.concatenate([keys, values], axis=1)
    padded = extended(key_value, (("nodes", 0),), SPAN)
    node_count = node_rows * lax.axis_size("nodes")
    first_node = lax.axis_index("nodes") * node_rows
    local_index = jnp.mod(neighbours - first_node + SPAN, node_count)
    places = local_index.T
    weights, mixed, inverse_sum = attend(places, queries, padded[:, :local_width], padded[:, local_width:].T)
    attn_share = lax.psum_scatter(
        jnp.dot(mixed, w_out, preferred_element_type=jnp.float32).astype(jnp.bfloat16),
        "heads",
        scatter_dimension=1,
        tiled=True,
    ).astype(jnp.float32)
    middle = inputs.astype(jnp.float32) + attn_share
    full_mid = lax.all_gather(middle.astype(jnp.bfloat16), "heads", axis=1, tiled=True).astype(
        middle.dtype
    )
    normed2, inverse2 = norm_full(full_mid)
    normed_two = (normed2 * (1.0 + level_rows(2)) + level_rows(3)).astype(jnp.bfloat16)
    pre_act = jnp.dot(normed_two, w_up, preferred_element_type=jnp.float32)
    activated = jax.nn.silu(pre_act).astype(jnp.bfloat16)
    mlp_share = lax.psum_scatter(
        jnp.dot(activated, w_down, preferred_element_type=jnp.float32).astype(jnp.bfloat16),
        "heads",
        scatter_dimension=1,
        tiled=True,
    ).astype(jnp.float32)
    output = (middle + mlp_share).astype(jnp.bfloat16)

    def norm_back(grad_share, normed_whole, inverse, which):
        normed_share = lax.dynamic_slice_in_dim(normed_whole, column_first, half, 1)
        scale_table = lax.dynamic_slice_in_dim(mod_table[2 * which], column_first, half, 1)
        scale_share = jnp.dot(onehot, scale_table, precision=highest)
        gained = grad_share * (1.0 + scale_share)
        sum_gain, sum_cross = lax.psum(
            (jnp.sum(gained, axis=1), jnp.sum(gained * normed_share, axis=1)), "heads"
        )
        grad_in = inverse * (
            gained - sum_gain[:, None] / width - normed_share * sum_cross[:, None] / width
        )
        grad_scale = contract_rows(onehot, grad_share * normed_share, highest)
        grad_shift = contract_rows(onehot, grad_share, highest)
        return (grad_in, grad_scale, grad_shift)

    full_cot = lax.all_gather(cotangent, "heads", axis=1, tiled=True)
    grad_down = contract_rows(activated, full_cot)
    grad_act = contract_cols(full_cot, w_down)
    sigma = jax.nn.sigmoid(pre_act)
    grad_pre = (grad_act * sigma * (1.0 + pre_act * (1.0 - sigma))).astype(jnp.bfloat16)
    grad_up = contract_rows(normed_two, grad_pre)
    grad_two = lax.psum_scatter(
        contract_cols(grad_pre, w_up).astype(jnp.bfloat16), "heads", scatter_dimension=1, tiled=True
    ).astype(jnp.float32)
    grad_in2, scale_two, shift_two = norm_back(grad_two, normed2, inverse2, 1)
    grad_mid = cotangent.astype(jnp.float32) + grad_in2
    grad_branch = lax.all_gather(grad_mid.astype(jnp.bfloat16), "heads", axis=1, tiled=True)
    grad_out = contract_rows(mixed, grad_branch)
    grad_t = dot(w_out, grad_branch, 1, 1)
    grad_queries, grad_key_pad, grad_value_pad = attend_back(
        weights, inverse_sum, queries, padded[:, :local_width].T, padded[:, local_width:], grad_t
    )
    grad_pad = jnp.concatenate([grad_key_pad, grad_value_pad], axis=1)
    from_above = passed_along(grad_pad[:SPAN].astype(jnp.bfloat16), "nodes", -1).astype(jnp.float32)
    from_below = passed_along(grad_pad[node_rows + SPAN :].astype(jnp.bfloat16), "nodes", 1).astype(
        jnp.float32
    )
    grad_centre = grad_pad[SPAN : SPAN + node_rows]
    grad_centre = grad_centre.at[:SPAN].add(from_below)
    grad_centre = grad_centre.at[node_rows - SPAN :].add(from_above)
    grad_keys = grad_centre[:, :local_width].astype(jnp.bfloat16)
    grad_values = grad_centre[:, local_width:].astype(jnp.bfloat16)
    grad_query = contract_rows(normed_one, grad_queries)
    grad_key = contract_rows(normed_one, grad_keys)
    grad_value = contract_rows(normed_one, grad_values)
    grad_joined = jnp.concatenate([grad_queries, grad_keys, grad_values], axis=1)
    weights_joined = jnp.concatenate([w_query, w_key, w_value], axis=1)
    grad_one = lax.psum_scatter(
        contract_cols(grad_joined, weights_joined).astype(jnp.bfloat16),
        "heads",
        scatter_dimension=1,
        tiled=True,
    ).astype(jnp.float32)
    grad_in1, scale_one, shift_one = norm_back(grad_one, normed1, inverse1, 0)
    grad_inputs = grad_mid + grad_in1
    grad_table = jnp.stack([scale_one, shift_one, scale_two, shift_two])
    up_total, down_total, query_total, key_total, value_total, out_total, table_total = lax.psum(
        (grad_up, grad_down, grad_query, grad_key, grad_value, grad_out, grad_table), "nodes"
    )
    return (
        output,
        grad_inputs,
        query_total,
        key_total,
        value_total,
        out_total,
        up_total,
        down_total,
        table_total,
    )


def solution(mesh):
    return jax.shard_map(
        body,
        mesh=mesh,
        in_specs=(
            P("nodes", "heads"),
            P(None, "heads"),
            P(None, "heads"),
            P(None, "heads"),
            P("heads", None),
            P(None, "heads"),
            P("heads", None),
            P(),
            P("nodes"),
            P("nodes", None),
            P("nodes", "heads"),
        ),
        out_specs=(
            P("nodes", "heads"),
            P("nodes", "heads"),
            P(None, "heads"),
            P(None, "heads"),
            P(None, "heads"),
            P("heads", None),
            P(None, "heads"),
            P("heads", None),
            P(None, None, "heads"),
        ),
        check_vma=False,
    )
```

```python
import math

import jax
import jax.numpy as jnp
from jax import lax
from jax.experimental import pallas as pl
from jax.experimental.pallas import tpu as pltpu
from jax.sharding import PartitionSpec as P

HD = 128
K = 16
SPAN = 896
ROWS = 128
WORD = 64
epsilon = 1e-05
highest = lax.Precision.HIGHEST
HUGE = -1e30
VMEM = 56 * 1024 * 1024


def dot(left, right, left_dim, right_dim):
    return lax.dot_general(
        left,
        right,
        (((left_dim,), (right_dim,)), ((), ())),
        preferred_element_type=jnp.float32,
    )


def two_blocks(first, second):
    zero = jnp.zeros_like(first)
    return jnp.concatenate(
        [jnp.concatenate([first, zero], 1), jnp.concatenate([zero, second], 1)], 0
    )


def forward_kernel(nbr_ref, q_ref, k_ref, vt_ref, e_ref, mixed_ref, inv_ref):
    block = pl.program_id(0)
    start = pl.multiple_of(block * ROWS, ROWS)
    window = e_ref.shape[1]
    factor = 1.0 / math.sqrt(HD)
    scale = factor * math.log2(math.e)
    place = nbr_ref[:, pl.ds(start, ROWS)] - start
    bit = jnp.left_shift(1, jnp.right_shift(place, 6))
    low = jnp.bitwise_and(place, WORD - 1)
    lane_low = lax.broadcasted_iota(jnp.int32, (WORD, ROWS), 0)
    words = jnp.zeros((WORD, ROWS), jnp.int32)
    for j in range(K):
        words = words | jnp.where(lane_low == low[j : j + 1, :], bit[j : j + 1, :], 0)
    words = jnp.concatenate([words, words], 1)
    queries = q_ref[pl.ds(start, ROWS), :]
    both = two_blocks(queries[:, :HD], queries[:, HD:])
    scores = dot(k_ref[pl.ds(start, window), :], both, 1, 1)
    masked = []
    for t in range(window // WORD):
        keep = (words & (1 << t)) != 0
        masked.append(jnp.where(keep, scores[t * WORD : (t + 1) * WORD, :], HUGE))
    top = masked[0]
    for part in masked[1:]:
        top = jnp.maximum(top, part)
    top = jnp.max(top, axis=0, keepdims=True) * scale
    total = jnp.zeros((WORD, 2 * ROWS), jnp.float32)
    weights = []
    for part in masked:
        weight = jnp.exp2(part * scale - top)
        total = total + weight
        weights.append(weight.astype(jnp.bfloat16))
    inverse = 1.0 / jnp.sum(total, axis=0, keepdims=True)
    weights = jnp.concatenate(weights, 0)
    e_ref[0] = weights
    inv_ref[0] = jnp.broadcast_to(inverse, inv_ref.shape[1:])
    mixed = dot(vt_ref[:, pl.ds(start, window)], weights, 1, 0) * inverse
    mixed_ref[:, :HD] = mixed[:HD, :ROWS].T.astype(jnp.bfloat16)
    mixed_ref[:, HD:] = mixed[HD:, ROWS:].T.astype(jnp.bfloat16)


def attend(places, queries, keys, values_t):
    rows = queries.shape[0]
    wide = 2 * HD
    blocks = rows // ROWS
    window = ROWS + 2 * SPAN
    return pl.pallas_call(
        forward_kernel,
        grid=(blocks,),
        in_specs=[
            pl.BlockSpec(places.shape, lambda b: (0, 0)),
            pl.BlockSpec(queries.shape, lambda b: (0, 0)),
            pl.BlockSpec(keys.shape, lambda b: (0, 0)),
            pl.BlockSpec(values_t.shape, lambda b: (0, 0)),
        ],
        out_specs=[
            pl.BlockSpec((1, window, wide), lambda b: (b, 0, 0)),
            pl.BlockSpec((ROWS, wide), lambda b: (b, 0)),
            pl.BlockSpec((1, 8, wide), lambda b: (b, 0, 0)),
        ],
        out_shape=[
            jax.ShapeDtypeStruct((blocks, window, wide), jnp.bfloat16),
            jax.ShapeDtypeStruct((rows, wide), jnp.bfloat16),
            jax.ShapeDtypeStruct((blocks, 8, wide), jnp.float32),
        ],
        compiler_params=pltpu.CompilerParams(vmem_limit_bytes=VMEM),
        name="attend_forward",
    )(places, queries, keys, values_t)


def backward_kernel(
    e_ref, inv_ref, q_ref, kt_ref, v_ref, gt_ref, dq_ref, dk_ref, dv_ref, dk_sum, dv_sum
):
    block = pl.program_id(0)
    start = pl.multiple_of(block * ROWS, ROWS)
    window = e_ref.shape[1]
    factor = 1.0 / math.sqrt(HD)

    @pl.when(block == 0)
    def _():
        dk_sum[...] = jnp.zeros_like(dk_sum)
        dv_sum[...] = jnp.zeros_like(dv_sum)

    inverse = inv_ref[0][:1, :]
    queries = q_ref[pl.ds(start, ROWS), :]
    both = two_blocks(queries[:, :HD], queries[:, HD:])
    grad = gt_ref[:, pl.ds(start, ROWS)]
    grad_both = two_blocks(
        (grad[:HD, :] * inverse[:, :ROWS]).astype(jnp.bfloat16),
        (grad[HD:, :] * inverse[:, ROWS:]).astype(jnp.bfloat16),
    )
    weights = e_ref[0]
    spots = pl.ds(start, window)
    grad_probs = dot(v_ref[spots, :], grad_both, 1, 0)
    wide = weights.astype(jnp.float32)
    cross = jnp.sum(grad_probs * wide, axis=0, keepdims=True) * inverse
    grad_scores = (wide * (grad_probs - cross)).astype(jnp.bfloat16)
    dv_sum[spots, :] += dot(weights, grad_both, 1, 1)
    dk_sum[spots, :] += dot(grad_scores, both, 1, 0)
    grad_query = dot(kt_ref[:, spots], grad_scores, 1, 0) * factor
    dq_ref[:, :HD] = grad_query[:HD, :ROWS].T.astype(jnp.bfloat16)
    dq_ref[:, HD:] = grad_query[HD:, ROWS:].T.astype(jnp.bfloat16)

    @pl.when(block == pl.num_programs(0) - 1)
    def _():
        dk_ref[...] = (dk_sum[...] * factor).astype(dk_ref.dtype)
        dv_ref[...] = dv_sum[...].astype(dv_ref.dtype)


def attend_back(weights, inverse, queries, keys_t, values, grad_t):
    rows = queries.shape[0]
    wide = 2 * HD
    blocks, window, _ = weights.shape
    span_rows = values.shape[0]
    whole = lambda array: pl.BlockSpec(array.shape, lambda b: (0, 0))
    return pl.pallas_call(
        backward_kernel,
        grid=(blocks,),
        in_specs=[
            pl.BlockSpec((1, window, wide), lambda b: (b, 0, 0)),
            pl.BlockSpec((1, 8, wide), lambda b: (b, 0, 0)),
            whole(queries),
            whole(keys_t),
            whole(values),
            whole(grad_t),
        ],
        out_specs=[
            pl.BlockSpec((ROWS, wide), lambda b: (b, 0)),
            pl.BlockSpec((span_rows, wide), lambda b: (0, 0)),
            pl.BlockSpec((span_rows, wide), lambda b: (0, 0)),
        ],
        out_shape=[
            jax.ShapeDtypeStruct((rows, wide), jnp.bfloat16),
            jax.ShapeDtypeStruct((span_rows, wide), jnp.float32),
            jax.ShapeDtypeStruct((span_rows, wide), jnp.float32),
        ],
        scratch_shapes=[
            pltpu.VMEM((span_rows, wide), jnp.float32),
            pltpu.VMEM((span_rows, wide), jnp.float32),
        ],
        compiler_params=pltpu.CompilerParams(vmem_limit_bytes=VMEM),
        name="attend_backward",
    )(weights, inverse, queries, keys_t, values, grad_t)


def passed_along(block, axis, distance):
    devices = range(lax.axis_size(axis))
    route = [((i - distance) % len(devices), i) for i in devices]
    return lax.ppermute(block, axis, route)


def swapped(block, axis, bit):
    devices = range(lax.axis_size(axis))
    return lax.ppermute(block, axis, [(i, i ^ bit) for i in devices])


def bits_of(axis, swap):
    bits = [1 << k for k in range(lax.axis_size(axis).bit_length() - 1)]
    if swap:
        bits[0], bits[1] = bits[1], bits[0]
    return bits


def scatter_sum(block, axis, bits):
    place = lax.axis_index(axis)
    for bit in bits:
        half = block.shape[0] // 2
        upper = (place & bit) != 0
        send = jnp.where(upper, block[:half], block[half:])
        keep = jnp.where(upper, block[half:], block[:half])
        got = swapped(send, axis, bit)
        block = (keep.astype(jnp.float32) + got.astype(jnp.float32)).astype(jnp.bfloat16)
    return block


def gathered(block, axis, bits):
    place = lax.axis_index(axis)
    for bit in reversed(bits):
        upper = (place & bit) != 0
        got = swapped(block, axis, bit)
        block = jnp.where(
            upper, jnp.concatenate([got, block]), jnp.concatenate([block, got])
        )
    return block


def total_of(block, axis, swap):
    bits = bits_of(axis, swap)
    return gathered(scatter_sum(block.astype(jnp.bfloat16), axis, bits), axis, bits)


def norm_full(values):
    row_mean = jnp.mean(values, axis=1, keepdims=True)
    centred = values - row_mean
    variance = jnp.mean(centred * centred, axis=1, keepdims=True)
    inverse = lax.rsqrt(variance + epsilon)
    return (centred * inverse, inverse)


def in_three(table):
    first = lax.reduce_precision(table, 8, 7)
    rest = table - first
    second = lax.reduce_precision(rest, 8, 7)
    return jnp.concatenate([first, second, rest - second], axis=0).astype(jnp.bfloat16)


def body(
    inputs,
    w_query,
    w_key,
    w_value,
    w_out,
    w_up,
    w_down,
    mod_table,
    level_ids,
    neighbours,
    cotangent,
):
    rows, half = inputs.shape
    width = half * lax.axis_size("heads")
    local_width = w_query.shape[1]
    levels = mod_table.shape[1]
    first_head = lax.axis_index("heads") == 0
    bf16 = jnp.bfloat16
    f32 = jnp.float32

    def mine(block):
        return jnp.where(first_head, block[:, :half], block[:, half:])

    def theirs(block):
        return jnp.where(first_head, block[:, half:], block[:, :half])

    def whole(block):
        return lax.all_gather(block, "heads", axis=1, tiled=True)

    before = passed_along(inputs, "nodes", 1)
    after = passed_along(inputs, "nodes", -1)
    levels_before = passed_along(level_ids, "nodes", 1)
    levels_after = passed_along(level_ids, "nodes", -1)
    full_in = whole(inputs)
    full_cot = whole(cotangent)
    full_around = whole(jnp.concatenate([before, after], axis=0))
    rows_in = jnp.concatenate([full_around[:rows], full_in, full_around[rows:]], axis=0)
    levels_all = jnp.concatenate([levels_before, level_ids, levels_after])

    def onehot_of(ids):
        return (ids[:, None] == jnp.arange(levels, dtype=jnp.int32)[None, :]).astype(bf16)

    onehot_all = onehot_of(levels_all)
    onehot = onehot_of(level_ids)
    tables = [in_three(mod_table[which]) for which in range(4)]

    def level_rows(chosen, which):
        return dot(jnp.concatenate([chosen] * 3, axis=1), tables[which], 1, 0)

    normed1, inverse1 = norm_full(rows_in.astype(f32))
    normed_all = (
        normed1 * (1.0 + level_rows(onehot_all, 0)) + level_rows(onehot_all, 1)
    ).astype(bf16)
    normed_one = normed_all[rows : 2 * rows]
    queries = dot(normed_one, w_query, 1, 0).astype(bf16)
    keys = dot(normed_all, w_key, 1, 0).astype(bf16)
    values_t = dot(w_value, normed_all, 0, 1).astype(bf16)
    keys_t = dot(w_key, normed_all, 0, 1).astype(bf16)
    values = dot(normed_all, w_value, 1, 0).astype(bf16)
    node_count = rows * lax.axis_size("nodes")
    first_node = lax.axis_index("nodes") * rows
    places = jnp.mod(neighbours.T - first_node + SPAN, node_count)
    weights, mixed, inverse_sum = attend(places, queries, keys, values_t)

    attn_part = dot(mixed, w_out, 1, 0).astype(bf16)
    attn_other = swapped(attn_part, "heads", 1)
    middle = full_in.astype(f32) + (attn_part.astype(f32) + attn_other.astype(f32))
    normed2, inverse2 = norm_full(middle)
    gain2 = 1.0 + level_rows(onehot, 2)
    normed_two = (normed2 * gain2 + level_rows(onehot, 3)).astype(bf16)
    pre_act = dot(normed_two, w_up, 1, 0)
    sigma = jax.nn.sigmoid(pre_act)
    activated = (pre_act * sigma).astype(bf16)
    grad_act = dot(full_cot, w_down, 1, 1)
    grad_pre = (grad_act * sigma * (1.0 + pre_act * (1.0 - sigma))).astype(bf16)
    two_part = dot(grad_pre, w_up, 1, 1).astype(bf16)
    two_other = swapped(two_part, "heads", 1)
    mlp_part = dot(activated, w_down, 1, 0)
    mlp_other = swapped(theirs(mlp_part).astype(bf16), "heads", 1)
    output = (mine(middle) + (mine(mlp_part) + mlp_other.astype(f32))).astype(bf16)
    grad_up = dot(normed_two, grad_pre, 0, 0)
    grad_down = dot(activated, full_cot, 0, 0)
    up_total = total_of(grad_up, "nodes", False).astype(f32)
    down_total = total_of(grad_down, "nodes", True).astype(f32)

    grad_two = two_part.astype(f32) + two_other.astype(f32)
    gained = grad_two * gain2
    grad_mid = full_cot.astype(f32) + inverse2 * (
        gained
        - jnp.mean(gained, axis=1, keepdims=True)
        - normed2 * jnp.mean(gained * normed2, axis=1, keepdims=True)
    )
    scale_two = dot(onehot, mine(grad_two * normed2).astype(bf16), 0, 0)
    shift_two = dot(onehot, mine(grad_two).astype(bf16), 0, 0)
    grad_branch = grad_mid.astype(bf16)
    grad_out = dot(mixed, grad_branch, 0, 0)
    grad_t = dot(w_out, grad_branch, 1, 1)
    grad_queries, grad_keys, grad_values = attend_back(
        weights, inverse_sum, queries, keys_t, values, grad_t
    )
    grad_keys = grad_keys.astype(bf16)
    grad_values = grad_values.astype(bf16)
    grad_query = dot(normed_one, grad_queries, 0, 0)
    grad_key = dot(normed_all, grad_keys, 0, 0)
    grad_value = dot(normed_all, grad_values, 0, 0)
    one_part = dot(
        jnp.concatenate([grad_keys, grad_values], axis=1),
        jnp.concatenate([w_key, w_value], axis=1),
        1,
        1,
    )
    one_part = one_part.at[rows : 2 * rows].add(dot(grad_queries, w_query, 1, 1))
    one_other = swapped(theirs(one_part).astype(bf16), "heads", 1)
    one_all = mine(one_part) + one_other.astype(f32)
    to_before = passed_along(one_all[:rows].astype(bf16), "nodes", -1)
    to_after = passed_along(one_all[2 * rows :].astype(bf16), "nodes", 1)
    normed1_mine = mine(normed1)
    scale_one = dot(onehot_all, (one_all * normed1_mine).astype(bf16), 0, 0)
    shift_one = dot(onehot_all, one_all.astype(bf16), 0, 0)
    first_set = jnp.concatenate([grad_query, grad_key], axis=0)
    table = jnp.concatenate([scale_one, shift_one, scale_two, shift_two], axis=0)
    second_set = jnp.concatenate(
        [grad_value, grad_out[:, :half], grad_out[:, half:], table, jnp.zeros_like(table)], axis=0
    )
    first_total = total_of(first_set, "nodes", False).astype(f32)
    second_total = total_of(second_set, "nodes", True).astype(f32)

    grad_one = (
        one_all[rows : 2 * rows] + to_before.astype(f32) + to_after.astype(f32)
    )
    normed_mine = normed1_mine[rows : 2 * rows]
    scale_mine = dot(
        jnp.concatenate([onehot] * 3, axis=1), mine(tables[0]), 1, 0
    )
    gained = grad_one * (1.0 + scale_mine)
    sum_gain, sum_cross = lax.psum(
        (jnp.sum(gained, axis=1), jnp.sum(gained * normed_mine, axis=1)), "heads"
    )
    grad_inputs = mine(grad_mid) + inverse1[rows : 2 * rows] * (
        gained - sum_gain[:, None] / width - normed_mine * sum_cross[:, None] / width
    )
    depth = w_query.shape[0]
    out_rows = w_out.shape[0]
    spots = [depth, depth + out_rows, depth + 2 * out_rows]
    return (
        output,
        grad_inputs,
        first_total[:depth],
        first_total[depth:],
        second_total[:depth],
        jnp.concatenate([second_total[spots[0] : spots[1]], second_total[spots[1] : spots[2]]], 1),
        up_total,
        down_total,
        second_total[spots[2] : spots[2] + 4 * levels].reshape(4, levels, half),
    )


def solution(mesh):
    return jax.shard_map(
        body,
        mesh=mesh,
        in_specs=(
            P("nodes", "heads"),
            P(None, "heads"),
            P(None, "heads"),
            P(None, "heads"),
            P("heads", None),
            P(None, "heads"),
            P("heads", None),
            P(),
            P("nodes"),
            P("nodes", None),
            P("nodes", "heads"),
        ),
        out_specs=(
            P("nodes", "heads"),
            P("nodes", "heads"),
            P(None, "heads"),
            P(None, "heads"),
            P(None, "heads"),
            P("heads", None),
            P(None, "heads"),
            P("heads", None),
            P(None, None, "heads"),
        ),
        check_vma=False,
    )
```

```python
import math

import jax
import jax.numpy as jnp
from jax import lax
from jax.experimental import pallas as pl
from jax.experimental.pallas import tpu as pltpu
from jax.sharding import PartitionSpec as P

HD = 128
K = 16
SPAN = 896
ROWS = 128
WORD = 64
HUGE = -1e30
MIB = 1024 * 1024
FRONT_MIB = 20
ATTEND_MIB = 24
MLP_MIB = 24
BRANCH_MIB = 20
BACK_MIB = 28
GRADS_MIB = 24
epsilon = 1e-05
bf16 = jnp.bfloat16
f32 = jnp.float32


def dot(left, right, left_dim, right_dim):
    return lax.dot_general(
        left,
        right,
        (((left_dim,), (right_dim,)), ((), ())),
        preferred_element_type=f32,
    )


def two_blocks(first, second):
    zero = jnp.zeros_like(first)
    return jnp.concatenate(
        [jnp.concatenate([first, zero], 1), jnp.concatenate([zero, second], 1)], 0
    )


def ordered(head, mine, theirs):
    return jnp.where(
        head == 0,
        jnp.concatenate([mine, theirs], axis=1),
        jnp.concatenate([theirs, mine], axis=1),
    )


def parted(head, block):
    half = block.shape[1] // 2
    low, high = block[:, :half], block[:, half:]
    return jnp.where(head == 0, low, high), jnp.where(head == 0, high, low)


def onehot_t(ids, levels):
    spots = lax.broadcasted_iota(jnp.int32, (levels, ids.shape[1]), 0)
    return jnp.where(spots == ids, 1.0, 0.0).astype(bf16)


def level_values(ids, table):
    chosen = onehot_t(ids, table.shape[0])
    first = table.astype(bf16)
    rest = table - first.astype(f32)
    second = rest.astype(bf16)
    third = (rest - second.astype(f32)).astype(bf16)
    return dot(
        jnp.concatenate([chosen] * 3, axis=0),
        jnp.concatenate([first, second, third], axis=0),
        0,
        0,
    )


def norm_rows(values):
    centred = values - jnp.mean(values, axis=1, keepdims=True)
    inverse = lax.rsqrt(jnp.mean(centred * centred, axis=1, keepdims=True) + epsilon)
    return centred * inverse, inverse


def cost(microseconds):
    return pl.CostEstimate(
        flops=int(microseconds * 5e8), bytes_accessed=int(microseconds * 2.5e6), transcendentals=0
    )


def call(kernel, name, microseconds, mebibytes, operands, out_shape, scratch=()):
    spaces = [
        pltpu.SMEM if operand.shape == (1,) else pltpu.VMEM for operand in operands
    ]
    return pl.pallas_call(
        kernel,
        in_specs=[pl.BlockSpec(memory_space=space) for space in spaces],
        out_shape=[jax.ShapeDtypeStruct(shape, kind) for shape, kind in out_shape],
        scratch_shapes=list(scratch),
        compiler_params=pltpu.CompilerParams(vmem_limit_bytes=mebibytes * MIB),
        cost_estimate=cost(microseconds),
        name=name,
    )(*operands)


def front_kernel(
    head_ref, ids_ref, mine_ref, theirs_ref, table_ref, key_ref, value_ref, *refs
):
    width = 2 * mine_ref.shape[1]
    more = len(refs) > 4
    normed_ref, unit_ref, k_ref, vt_ref = refs[-4:] if not more else refs[1:5]
    values = ordered(head_ref[0], mine_ref[...], theirs_ref[...]).astype(f32)
    unit, _ = norm_rows(values)
    level = level_values(
        ids_ref[...], jnp.concatenate([table_ref[0], table_ref[1]], axis=1)
    )
    normed = (unit * (1.0 + level[:, :width]) + level[:, width:]).astype(bf16)
    normed_ref[...] = normed
    unit_ref[...] = unit.astype(bf16)
    k_ref[...] = dot(normed, key_ref[...], 1, 0).astype(bf16)
    vt_ref[...] = dot(value_ref[...], normed, 0, 1).astype(bf16)
    if more:
        query_ref, (q_ref, kt_ref, v_ref) = refs[0], refs[5:]
        q_ref[...] = dot(normed, query_ref[...], 1, 0).astype(bf16)
        kt_ref[...] = dot(key_ref[...], normed, 0, 1).astype(bf16)
        v_ref[...] = dot(normed, value_ref[...], 1, 0).astype(bf16)


def front(head, ids, mine, theirs, table, w_key, w_value, *w_query):
    rows = mine.shape[0]
    width = 2 * mine.shape[1]
    wide = 2 * HD
    down, along = ((rows, wide), bf16), ((wide, rows), bf16)
    shapes = [((rows, width), bf16)] * 2 + [down, along]
    if w_query:
        shapes += [down, along, down]
    operands = (head, ids, mine, theirs, table, w_key, w_value, *w_query)
    return call(front_kernel, "front", 3, FRONT_MIB, operands, shapes)


def forward_kernel(
    nbr_ref, k0, k1, k2, vt0, vt1, vt2, q_ref, out_ref,
    e_ref, mixed_ref, inv_ref, part_ref, k_all, vt_all, s_new, s_old, top_old,
):
    blocks, window, _ = e_ref.shape
    rows = k0.shape[0]
    scale = math.log2(math.e) / math.sqrt(HD)
    for i, (k, vt) in enumerate(((k0, vt0), (k1, vt1), (k2, vt2))):
        k_all[i * rows : (i + 1) * rows, :] = k[...]
        vt_all[:, i * rows : (i + 1) * rows] = vt[...]
    s_old[...] = jnp.zeros_like(s_old)
    top_old[...] = jnp.zeros_like(top_old)

    def work(step, carry):
        old_block = jnp.maximum(step - 1, 0)
        start = pl.multiple_of(jnp.minimum(step, blocks - 1) * ROWS, ROWS)
        old_start = pl.multiple_of(old_block * ROWS, ROWS)
        place = nbr_ref[:, pl.ds(start, ROWS)] - start
        bit = jnp.left_shift(1, jnp.right_shift(place, 6))
        low = jnp.bitwise_and(place, WORD - 1)
        lane_low = lax.broadcasted_iota(jnp.int32, (WORD, ROWS), 0)
        words = jnp.zeros((WORD, ROWS), jnp.int32)
        for j in range(K):
            words = words | jnp.where(lane_low == low[j : j + 1, :], bit[j : j + 1, :], 0)
        queries = q_ref[pl.ds(start, ROWS), :]
        both = two_blocks(queries[:, :HD], queries[:, HD:])
        scores = dot(k_all[pl.ds(start, window), :], both, 1, 1)
        old = top_old[:1, :]
        top = None
        total = jnp.zeros((WORD, 2 * ROWS), f32)
        weights = []
        for t in range(window // WORD):
            there = slice(t * WORD, (t + 1) * WORD)
            keep = (words & (1 << t)) != 0
            part = scores[there, :]
            part = jnp.concatenate(
                [jnp.where(keep, part[:, :ROWS], HUGE), jnp.where(keep, part[:, ROWS:], HUGE)], 1
            )
            top = part if top is None else jnp.maximum(top, part)
            s_new[there, :] = part
            weight = jnp.exp2(s_old[there, :] * scale - old)
            total = total + weight
            weights.append(weight.astype(bf16))
        inverse = 1.0 / jnp.sum(total, axis=0, keepdims=True)
        weights = jnp.concatenate(weights, 0)
        e_ref[old_block] = weights
        there = pl.ds(old_start, ROWS)
        inv_ref[0:1, there] = inverse[:, :ROWS]
        inv_ref[1:2, there] = inverse[:, ROWS:]
        mixed = dot(vt_all[:, pl.ds(old_start, window)], weights, 1, 0) * inverse
        mixed = jnp.concatenate([mixed[:HD, :ROWS], mixed[HD:, ROWS:]], axis=0)
        mixed_ref[:, there] = mixed.astype(bf16)
        part_ref[there, :] = dot(mixed.T.astype(bf16), out_ref[...], 1, 0).astype(bf16)
        s_old[...] = s_new[...]
        top_old[...] = jnp.broadcast_to(jnp.max(top, axis=0, keepdims=True) * scale, top_old.shape)
        return carry

    lax.fori_loop(0, blocks + 1, work, 0)


def attend(places, keys, values_t, queries, w_out):
    rows = queries.shape[0]
    wide = 2 * HD
    blocks = rows // ROWS
    window = ROWS + 2 * SPAN
    shapes = [
        ((blocks, window, wide), bf16),
        ((wide, rows), bf16),
        ((8, rows), f32),
        ((rows, w_out.shape[1]), bf16),
    ]
    scratch = [
        pltpu.VMEM((3 * rows, wide), bf16),
        pltpu.VMEM((wide, 3 * rows), bf16),
        pltpu.VMEM((window, wide), f32),
        pltpu.VMEM((window, wide), f32),
        pltpu.VMEM((8, wide), f32),
    ]
    operands = (places, *keys, *values_t, queries, w_out)
    return call(forward_kernel, "attend_forward", 10, ATTEND_MIB, operands, shapes, scratch)


def mlp_kernel(
    head_ref, ids_ref, xm_ref, xt_ref, part_ref, other_ref, grad_ref, table_ref, up_ref, down_ref,
    middle_ref, two_ref, theirs_ref, out_ref, normed_ref, act_ref, pre_ref,
):
    head = head_ref[0]
    width = 2 * xm_ref.shape[1]
    values = ordered(head, xm_ref[...], xt_ref[...]).astype(f32)
    middle = values + (part_ref[...].astype(f32) + other_ref[...].astype(f32))
    middle_ref[...] = middle
    unit, _ = norm_rows(middle)
    level = level_values(
        ids_ref[...], jnp.concatenate([table_ref[2], table_ref[3]], axis=1)
    )
    normed = (unit * (1.0 + level[:, :width]) + level[:, width:]).astype(bf16)
    normed_ref[...] = normed
    pre = dot(normed, up_ref[...], 1, 0)
    sigma = jax.nn.sigmoid(pre)
    act = (pre * sigma).astype(bf16)
    act_ref[...] = act
    grad = grad_ref[...].astype(f32)
    grad = (grad * sigma * (1.0 + pre * (1.0 - sigma))).astype(bf16)
    pre_ref[...] = grad
    two_ref[...] = dot(grad, up_ref[...], 1, 1).astype(bf16)
    mine, theirs = parted(head, dot(act, down_ref[...], 1, 0))
    theirs_ref[...] = theirs.astype(bf16)
    out_ref[...] = parted(head, middle)[0] + mine


def mlp(head, ids, x_mine, x_theirs, part, other, grad_act, table, w_up, w_down):
    rows, half = x_mine.shape
    hidden = w_up.shape[1]
    shapes = [
        (2 * half, f32), (2 * half, bf16), (half, bf16), (half, f32),
        (2 * half, bf16), (hidden, bf16), (hidden, bf16),
    ]
    shapes = [((rows, wide), kind) for wide, kind in shapes]
    operands = (head, ids, x_mine, x_theirs, part, other, grad_act, table, w_up, w_down)
    return call(mlp_kernel, "mlp", 5, MLP_MIB, operands, shapes)


def branch_kernel(
    head_ref, ids_ref, middle_ref, cm_ref, ct_ref, two_ref, other_ref, mixed_ref, inv_ref, table_ref, out_ref,
    mid_ref, gout_ref, tab_ref, grad_ref, cross_ref,
):
    head = head_ref[0]
    ids = ids_ref[...]
    unit, inverse = norm_rows(middle_ref[...])
    gain = 1.0 + level_values(ids, table_ref[2])
    grad_two = two_ref[...].astype(f32) + other_ref[...].astype(f32)
    gained = grad_two * gain
    cot = ordered(head, cm_ref[...], ct_ref[...]).astype(f32)
    grad_mid = cot + inverse * (
        gained
        - jnp.mean(gained, axis=1, keepdims=True)
        - unit * jnp.mean(gained * unit, axis=1, keepdims=True)
    )
    mid_ref[...] = parted(head, grad_mid)[0]
    branch = grad_mid.astype(bf16)
    grad = dot(out_ref[...], branch, 1, 1)
    cross = grad * mixed_ref[...].astype(f32)
    for h in range(grad.shape[0] // HD):
        there = slice(h * HD, (h + 1) * HD)
        total = inv_ref[h : h + 1, :]
        grad_ref[there, :] = (grad[there, :] * total).astype(bf16)
        cross_ref[h : h + 1, :] = jnp.sum(cross[there, :], axis=0, keepdims=True) * total
    gout_ref[...] = dot(mixed_ref[...], branch, 1, 0).astype(bf16)
    tab_ref[...] = dot(
        onehot_t(ids, table_ref.shape[1]),
        jnp.concatenate(
            [parted(head, grad_two * unit)[0], parted(head, grad_two)[0]], 1
        ).astype(bf16),
        1,
        0,
    )


def branch(
    head, ids, middle, cot_mine, cot_theirs, two_part, two_other, mixed_t, inverse,
    table, w_out,
):
    rows, half = cot_mine.shape
    width = 2 * half
    shapes = [
        ((rows, half), f32),
        ((w_out.shape[0], width), bf16),
        ((table.shape[1], width), f32),
        ((2 * HD, rows), bf16),
        ((8, rows), f32),
    ]
    operands = (
        head, ids, middle, cot_mine, cot_theirs, two_part, two_other, mixed_t, inverse,
        table, w_out,
    )
    return call(branch_kernel, "branch", 3, BRANCH_MIB, operands, shapes)


def backward_kernel(
    e_ref, grad_ref, cross_ref, q_ref, v0, v1, v2, kt0, kt1, kt2,
    dkv_ref, dq_ref, dkv_sum, kt_all, v_all, ds_slots,
):
    blocks, window, wide = e_ref.shape
    rows = v0.shape[0]
    factor = 1.0 / math.sqrt(HD)
    dkv_sum[...] = jnp.zeros_like(dkv_sum)
    for i, (v, kt) in enumerate(((v0, kt0), (v1, kt1), (v2, kt2))):
        v_all[i * rows : (i + 1) * rows, :] = v[...]
        kt_all[:, i * rows : (i + 1) * rows] = kt[...]

    def scores_and_values(block):
        start = pl.multiple_of(block * ROWS, ROWS)
        grad = grad_ref[:, pl.ds(start, ROWS)]
        grad_both = two_blocks(grad[:HD, :], grad[HD:, :])
        cross = jnp.concatenate(
            [cross_ref[0:1, pl.ds(start, ROWS)], cross_ref[1:2, pl.ds(start, ROWS)]], axis=1
        )
        weights = e_ref[block]
        spots = pl.ds(start, window)
        grad_probs = dot(v_all[spots, :], grad_both, 1, 0)
        ds_slots[block % 2] = (weights.astype(f32) * (grad_probs - cross)).astype(bf16)
        dkv_sum[spots, wide:] += dot(weights, grad_both, 1, 1)

    def keys_and_queries(block):
        start = pl.multiple_of(block * ROWS, ROWS)
        spots = pl.ds(start, window)
        queries = q_ref[pl.ds(start, ROWS), :]
        both = two_blocks(queries[:, :HD], queries[:, HD:])
        grad_scores = ds_slots[block % 2]
        dkv_sum[spots, :wide] += dot(grad_scores, both, 1, 0)
        grad_query = dot(kt_all[:, spots], grad_scores, 1, 0) * factor
        dq_ref[pl.ds(start, ROWS), :HD] = grad_query[:HD, :ROWS].T.astype(bf16)
        dq_ref[pl.ds(start, ROWS), HD:] = grad_query[HD:, ROWS:].T.astype(bf16)

    def work(block, carry):
        scores_and_values(block)
        keys_and_queries(block - 1)
        return carry

    scores_and_values(0)
    lax.fori_loop(1, blocks, work, 0)
    keys_and_queries(blocks - 1)
    for i in range(3):
        there = slice(i * rows, (i + 1) * rows)
        dkv_ref[there, :wide] = (dkv_sum[there, :wide] * factor).astype(bf16)
        dkv_ref[there, wide:] = dkv_sum[there, wide:].astype(bf16)


def backward(weights, grad_t, cross, queries, values, keys_t):
    rows = queries.shape[0]
    wide = 2 * HD
    window = weights.shape[1]
    shapes = [((3 * rows, 2 * wide), bf16), ((rows, wide), bf16)]
    scratch = [
        pltpu.VMEM((3 * rows, 2 * wide), f32),
        pltpu.VMEM((wide, 3 * rows), bf16),
        pltpu.VMEM((3 * rows, wide), bf16),
        pltpu.VMEM((2, window, wide), bf16),
    ]
    operands = (weights, grad_t, cross, queries, *values, *keys_t)
    return call(backward_kernel, "attend_backward", 12, BACK_MIB, operands, shapes, scratch)


def grads_kernel(
    head_ref, dkv_ref, dq_ref, id0, id1, id2, n0, n1, n2, u0, u1, u2, key_ref, value_ref, query_ref,
    gq_ref, gkv_ref, mine_ref, theirs_ref, tab_mine, tab_theirs,
):
    head = head_ref[0]
    rows, width = n0.shape
    wide = dq_ref.shape[1]
    levels = tab_mine.shape[0]
    w_kv = jnp.concatenate([key_ref[...], value_ref[...]], axis=1)
    grad_kv = jnp.zeros((width, 2 * wide), f32)
    table_sum = jnp.zeros((levels, 2 * width), f32)
    for i, (ids, normed, units) in enumerate(((id0, n0, u0), (id1, n1, u1), (id2, n2, u2))):
        there = slice(i * rows, (i + 1) * rows)
        dkv = dkv_ref[there, :]
        grad_kv = grad_kv + dot(normed[...], dkv, 0, 0)
        part = dot(dkv, w_kv, 1, 1)
        if i == 1:
            part = part + dot(dq_ref[...], query_ref[...], 1, 1)
        mine, theirs = parted(head, part)
        mine_ref[there, :] = mine.astype(bf16)
        theirs_ref[there, :] = theirs.astype(bf16)
        table_sum = table_sum + dot(
            onehot_t(ids[...], levels),
            jnp.concatenate([part * units[...].astype(f32), part], 1).astype(bf16),
            1,
            0,
        )
    gkv_ref[...] = grad_kv.astype(bf16)
    gq_ref[...] = dot(n1[...], dq_ref[...], 0, 0).astype(bf16)
    scale_mine, scale_theirs = parted(head, table_sum[:, :width])
    shift_mine, shift_theirs = parted(head, table_sum[:, width:])
    tab_mine[...] = jnp.concatenate([scale_mine, shift_mine], axis=1)
    tab_theirs[...] = jnp.concatenate([scale_theirs, shift_theirs], axis=1)


def grads(head, dkv, dq, ids, normed, units, w_key, w_value, w_query, levels):
    rows, width = normed[0].shape
    half = width // 2
    wide = dq.shape[1]
    shapes = [
        ((width, wide), bf16),
        ((width, 2 * wide), bf16),
        ((3 * rows, half), bf16),
        ((3 * rows, half), bf16),
        ((levels, width), f32),
        ((levels, width), f32),
    ]
    operands = (head, dkv, dq, *ids, *normed, *units, w_key, w_value, w_query)
    return call(grads_kernel, "grads", 5, GRADS_MIB, operands, shapes)


def passed_along(block, axis, distance):
    devices = range(lax.axis_size(axis))
    route = [((i - distance) % len(devices), i) for i in devices]
    return lax.ppermute(block, axis, route)


def swapped(block, axis, bit):
    devices = range(lax.axis_size(axis))
    return lax.ppermute(block, axis, [(i, i ^ bit) for i in devices])


def held_until(block, *others):
    return lax.optimization_barrier((block, *others))[0]


def two_parts(block, axis, bit):
    half = block.shape[0] // 2
    upper = (lax.axis_index(axis) & bit) != 0
    send = jnp.where(upper, block[:half], block[half:])
    keep = jnp.where(upper, block[half:], block[:half])
    return send, keep


def added(keep, got):
    return (keep.astype(f32) + got.astype(f32)).astype(bf16)


def doubled(block, axis, bit):
    upper = (lax.axis_index(axis) & bit) != 0
    got = swapped(block, axis, bit)
    return jnp.where(upper, jnp.concatenate([got, block]), jnp.concatenate([block, got]))


def far_bits(axis):
    return [1 << k for k in range(2, lax.axis_size(axis).bit_length() - 1)]


def halved(block, axis, bit, *others):
    send, keep = two_parts(block, axis, bit)
    return added(keep, held_until(swapped(send, axis, bit), *others))


def scatter_far(block, axis, *others):
    for bit in far_bits(axis):
        block = halved(block, axis, bit, *others)
    return block


def gather_far(block, axis):
    for bit in reversed(far_bits(axis)):
        block = doubled(block, axis, bit)
    return block


def gather_near(first, second, axis):
    first, second = doubled(first, axis, 2), doubled(second, axis, 1)
    return doubled(first, axis, 1), doubled(second, axis, 2)


def body(
    inputs,
    w_query,
    w_key,
    w_value,
    w_out,
    w_up,
    w_down,
    mod_table,
    level_ids,
    neighbours,
    cotangent,
):
    rows, half = inputs.shape
    width = half * lax.axis_size("heads")
    levels = mod_table.shape[1]
    head = lax.axis_index("heads").astype(jnp.int32).reshape(1)
    first_head = lax.axis_index("heads") == 0
    ids_own = level_ids[None, :]

    before = passed_along(inputs, "nodes", 1)
    after = passed_along(inputs, "nodes", -1)
    in_other = swapped(inputs, "heads", 1)
    cot_other = swapped(cotangent, "heads", 1)
    own = front(head, ids_own, inputs, in_other, mod_table, w_key, w_value, w_query)
    queries, keys_t1, values1 = own[4:]
    ids_late = held_until(ids_own, own[0])
    ids_before = passed_along(ids_late, "nodes", 1)
    ids_after = passed_along(ids_late, "nodes", -1)
    node_count = rows * lax.axis_size("nodes")
    first_node = lax.axis_index("nodes") * rows
    places = jnp.mod(neighbours.T - first_node + SPAN, node_count)
    full_cot = jnp.where(
        first_head,
        jnp.concatenate([cotangent, cot_other], axis=1),
        jnp.concatenate([cot_other, cotangent], axis=1),
    )
    grad_act = dot(full_cot, w_down, 1, 1).astype(bf16)
    before_other = swapped(held_until(before, own[0], grad_act), "heads", 1)
    low = front(head, ids_before, before, before_other, mod_table, w_key, w_value)
    after_other = swapped(after, "heads", 1)
    high = front(head, ids_after, after, after_other, mod_table, w_key, w_value)
    normed, units, keys, values_t = zip(low, own[:4], high)
    weights, mixed_t, inverse, attn_part = attend(places, keys, values_t, queries, w_out)
    attn_other = swapped(attn_part, "heads", 1)
    middle, two_part, mlp_theirs, out_mine, normed_two, activated, grad_pre = mlp(
        head, ids_own, inputs, in_other, attn_part, attn_other, grad_act, mod_table, w_up, w_down
    )
    two_other = swapped(two_part, "heads", 1)
    grad_up = dot(normed_two, grad_pre, 0, 0).astype(bf16)
    grad_down = dot(activated, full_cot, 0, 0).astype(bf16)
    hidden = grad_up.shape[1] // 2
    grad_up = jnp.concatenate([grad_up[:, :hidden], grad_up[:, hidden:]])
    up_send, up_keep = two_parts(grad_up, "nodes", 1)
    down_send, down_keep = two_parts(grad_down, "nodes", 2)
    up_got = swapped(up_send, "nodes", 1)
    down_got = swapped(down_send, "nodes", 2)
    mlp_other = swapped(mlp_theirs, "heads", 1)
    output = (out_mine + mlp_other.astype(f32)).astype(bf16)

    keys_t = [
        dot(w_key, normed[0], 0, 1).astype(bf16),
        keys_t1,
        dot(w_key, normed[2], 0, 1).astype(bf16),
    ]
    values = [
        dot(normed[0], w_value, 1, 0).astype(bf16),
        values1,
        dot(normed[2], w_value, 1, 0).astype(bf16),
    ]
    mid_mine, grad_out, tab_two, grad_t, cross = branch(
        head, ids_own, middle, cotangent, cot_other, two_part, two_other, mixed_t, inverse,
        mod_table, w_out,
    )
    grad_t = held_until(grad_t, up_send, down_send)
    dkv, dq = backward(weights, grad_t, cross, queries, values, keys_t)
    up_send, up_keep = two_parts(added(up_keep, held_until(up_got, dq)), "nodes", 2)
    down_send, down_keep = two_parts(added(down_keep, held_until(down_got, dq)), "nodes", 1)
    up_got = swapped(up_send, "nodes", 2)
    down_got = swapped(down_send, "nodes", 1)
    dq = held_until(dq, up_send, down_send)
    grad_q, grad_kv, one_mine, one_theirs, tab_mine, tab_theirs = grads(
        head, dkv, dq, (ids_before, ids_own, ids_after), normed, units,
        w_key, w_value, w_query, levels,
    )
    tab_other = swapped(tab_theirs, "heads", 1)
    one_other = swapped(one_theirs, "heads", 1)
    one_all = one_mine.astype(f32) + one_other.astype(f32)
    to_before = passed_along(one_all[:rows].astype(bf16), "nodes", -1)
    to_after = passed_along(one_all[2 * rows :].astype(bf16), "nodes", 1)
    wide = grad_q.shape[1]
    out_rows = grad_out.shape[0]
    spare = -(width + 2 * levels) % max(64, lax.axis_size("nodes"))
    table = jnp.concatenate([tab_mine + tab_other, tab_two], axis=0).astype(bf16)
    q_and_k = jnp.concatenate([grad_q, grad_kv[:, :wide]], axis=1)
    v_and_more = jnp.concatenate(
        [
            jnp.concatenate(
                [
                    grad_kv[:, wide:],
                    jnp.concatenate([grad_out[:, :half], grad_out[:, half:]], axis=0),
                ],
                axis=1,
            ),
            table,
            jnp.zeros((spare, width), bf16),
        ],
        axis=0,
    )
    qk_send, qk_keep = two_parts(q_and_k, "nodes", 1)
    qk_got = swapped(qk_send, "nodes", 1)
    up_sum = added(up_keep, held_until(up_got, qk_send))
    down_sum = added(down_keep, held_until(down_got, qk_send))
    mlp_sum = jnp.concatenate([up_sum, down_sum])
    mlp_sum = halved(mlp_sum, "nodes", 4, one_all)
    more_sum = halved(v_and_more, "nodes", 2)
    qk_sum = added(qk_keep, held_until(qk_got, one_all))
    qk_sum, more_sum = halved(qk_sum, "nodes", 2), halved(more_sum, "nodes", 1)
    for bit in far_bits("nodes")[1:]:
        mlp_sum = halved(mlp_sum, "nodes", bit)
    attn_sum = scatter_far(jnp.concatenate([qk_sum, more_sum]), "nodes")
    mlp_sum = held_until(mlp_sum, to_before, to_after)
    mlp_sum = gather_far(mlp_sum, "nodes")
    up_total, down_total = gather_near(
        mlp_sum[: mlp_sum.shape[0] // 2], mlp_sum[mlp_sum.shape[0] // 2 :], "nodes"
    )
    attn_sum = gather_far(attn_sum, "nodes")
    count = qk_sum.shape[0]
    qk_total, more_total = gather_near(attn_sum[:count], attn_sum[count:], "nodes")

    grad_one = one_all[rows : 2 * rows] + to_before.astype(f32) + to_after.astype(f32)
    full_in = jnp.concatenate([inputs, in_other], axis=1).astype(f32)
    unit, inverse = norm_rows(full_in)
    unit = unit[:, :half]
    onehot = (level_ids[:, None] == jnp.arange(levels, dtype=jnp.int32)[None, :]).astype(f32)
    scale_mine = jnp.where(first_head, mod_table[0][:, :half], mod_table[0][:, half:])
    gain = 1.0 + jnp.dot(onehot, scale_mine, precision=lax.Precision.HIGHEST)
    gained = grad_one * gain
    sum_gain, sum_cross = lax.psum(
        (jnp.sum(gained, axis=1), jnp.sum(gained * unit, axis=1)), "heads"
    )
    grad_inputs = mid_mine + inverse * (
        gained - sum_gain[:, None] / width - unit * sum_cross[:, None] / width
    )
    depth = w_query.shape[0]
    table_total = more_total[depth : depth + 2 * levels].astype(f32)
    return (
        output,
        grad_inputs,
        qk_total[:, :wide].astype(f32),
        qk_total[:, wide:].astype(f32),
        more_total[:depth, :wide].astype(f32),
        jnp.concatenate(
            [more_total[:out_rows, wide:], more_total[out_rows:depth, wide:]], axis=1
        ).astype(f32),
        jnp.concatenate([up_total[: width], up_total[width:]], axis=1).astype(f32),
        down_total.astype(f32),
        jnp.stack(
            [
                table_total[:levels, :half],
                table_total[:levels, half:],
                table_total[levels:, :half],
                table_total[levels:, half:],
            ]
        ),
    )


def solution(mesh):
    return jax.shard_map(
        body,
        mesh=mesh,
        in_specs=(
            P("nodes", "heads"),
            P(None, "heads"),
            P(None, "heads"),
            P(None, "heads"),
            P("heads", None),
            P(None, "heads"),
            P("heads", None),
            P(),
            P("nodes"),
            P("nodes", None),
            P("nodes", "heads"),
        ),
        out_specs=(
            P("nodes", "heads"),
            P("nodes", "heads"),
            P(None, "heads"),
            P(None, "heads"),
            P(None, "heads"),
            P("heads", None),
            P(None, "heads"),
            P("heads", None),
            P(None, None, "heads"),
        ),
        check_vma=False,
    )
```

```python
import math

import jax
import jax.numpy as jnp
from jax import lax
from jax.experimental import pallas as pl
from jax.experimental.pallas import tpu as pltpu
from jax.sharding import PartitionSpec as P

HD = 128
K = 16
SPAN = 896
ROWS = 128
WORD = 64
HUGE = -1e30
MIB = 1024 * 1024
FRONT_MIB = 20
ATTEND_MIB = 24
MLP_MIB = 28
BRANCH_MIB = 14
BACK_MIB = 28
GRADS_MIB = 24
UNPACK_MIB = 8
epsilon = 1e-05
bf16 = jnp.bfloat16
f32 = jnp.float32


def dot(left, right, left_dim, right_dim):
    return lax.dot_general(
        left,
        right,
        (((left_dim,), (right_dim,)), ((), ())),
        preferred_element_type=f32,
    )


def two_blocks(first, second):
    zero = jnp.zeros_like(first)
    return jnp.concatenate(
        [jnp.concatenate([first, zero], 1), jnp.concatenate([zero, second], 1)], 0
    )


def ordered(head, mine, theirs):
    return jnp.where(
        head == 0,
        jnp.concatenate([mine, theirs], axis=1),
        jnp.concatenate([theirs, mine], axis=1),
    )


def parted(head, block):
    half = block.shape[1] // 2
    low, high = block[:, :half], block[:, half:]
    return jnp.where(head == 0, low, high), jnp.where(head == 0, high, low)


def onehot_t(ids, levels):
    spots = lax.broadcasted_iota(jnp.int32, (levels, ids.shape[1]), 0)
    return jnp.where(spots == ids, 1.0, 0.0).astype(bf16)


def level_values(ids, table):
    chosen = onehot_t(ids, table.shape[0])
    first = table.astype(bf16)
    rest = table - first.astype(f32)
    second = rest.astype(bf16)
    third = (rest - second.astype(f32)).astype(bf16)
    return dot(
        jnp.concatenate([chosen] * 3, axis=0),
        jnp.concatenate([first, second, third], axis=0),
        0,
        0,
    )


def norm_rows(values):
    centred = values - jnp.mean(values, axis=1, keepdims=True)
    inverse = lax.rsqrt(jnp.mean(centred * centred, axis=1, keepdims=True) + epsilon)
    return centred * inverse, inverse


def cost(microseconds):
    return pl.CostEstimate(
        flops=int(microseconds * 5e8), bytes_accessed=int(microseconds * 2.5e6), transcendentals=0
    )


def call(kernel, name, microseconds, mebibytes, operands, out_shape, scratch=()):
    spaces = [
        pltpu.SMEM if operand.shape == (1,) else pltpu.VMEM for operand in operands
    ]
    return pl.pallas_call(
        kernel,
        in_specs=[pl.BlockSpec(memory_space=space) for space in spaces],
        out_shape=[jax.ShapeDtypeStruct(shape, kind) for shape, kind in out_shape],
        scratch_shapes=list(scratch),
        compiler_params=pltpu.CompilerParams(vmem_limit_bytes=mebibytes * MIB),
        cost_estimate=cost(microseconds),
        name=name,
    )(*operands)


def front_kernel(
    head_ref, ids_ref, mine_ref, theirs_ref, table_ref, key_ref, value_ref, *refs
):
    width = 2 * mine_ref.shape[1]
    more = len(refs) > 4
    normed_ref, unit_ref, k_ref, vt_ref = refs[-4:] if not more else refs[1:5]
    values = ordered(head_ref[0], mine_ref[...], theirs_ref[...]).astype(f32)
    unit, _ = norm_rows(values)
    level = level_values(
        ids_ref[...], jnp.concatenate([table_ref[0], table_ref[1]], axis=1)
    )
    normed = (unit * (1.0 + level[:, :width]) + level[:, width:]).astype(bf16)
    normed_ref[...] = normed
    unit_ref[...] = unit.astype(bf16)
    k_ref[...] = dot(normed, key_ref[...], 1, 0).astype(bf16)
    vt_ref[...] = dot(value_ref[...], normed, 0, 1).astype(bf16)
    if more:
        query_ref, (q_ref, kt_ref, v_ref) = refs[0], refs[5:]
        q_ref[...] = dot(normed, query_ref[...], 1, 0).astype(bf16)
        kt_ref[...] = dot(key_ref[...], normed, 0, 1).astype(bf16)
        v_ref[...] = dot(normed, value_ref[...], 1, 0).astype(bf16)


def front(head, ids, mine, theirs, table, w_key, w_value, *w_query):
    rows = mine.shape[0]
    width = 2 * mine.shape[1]
    wide = 2 * HD
    down, along = ((rows, wide), bf16), ((wide, rows), bf16)
    shapes = [((rows, width), bf16)] * 2 + [down, along]
    if w_query:
        shapes += [down, along, down]
    operands = (head, ids, mine, theirs, table, w_key, w_value, *w_query)
    return call(front_kernel, "front", 6.30, FRONT_MIB, operands, shapes)


def forward_kernel(
    nbr_ref, k0, k1, k2, vt0, vt1, vt2, q_ref, out_ref,
    e_ref, mixed_ref, inv_ref, part_ref, k_all, vt_all, s_new, s_old, top_old,
):
    blocks, window, _ = e_ref.shape
    rows = k0.shape[0]
    scale = math.log2(math.e) / math.sqrt(HD)
    for i, (k, vt) in enumerate(((k0, vt0), (k1, vt1), (k2, vt2))):
        k_all[i * rows : (i + 1) * rows, :] = k[...]
        vt_all[:, i * rows : (i + 1) * rows] = vt[...]
    s_old[...] = jnp.zeros_like(s_old)
    top_old[...] = jnp.zeros_like(top_old)

    def work(step, carry):
        old_block = jnp.maximum(step - 1, 0)
        start = pl.multiple_of(jnp.minimum(step, blocks - 1) * ROWS, ROWS)
        old_start = pl.multiple_of(old_block * ROWS, ROWS)
        place = nbr_ref[:, pl.ds(start, ROWS)] - start
        bit = jnp.left_shift(1, jnp.right_shift(place, 6))
        low = jnp.bitwise_and(place, WORD - 1)
        lane_low = lax.broadcasted_iota(jnp.int32, (WORD, ROWS), 0)
        words = jnp.zeros((WORD, ROWS), jnp.int32)
        for j in range(K):
            words = words | jnp.where(lane_low == low[j : j + 1, :], bit[j : j + 1, :], 0)
        queries = q_ref[pl.ds(start, ROWS), :]
        both = two_blocks(queries[:, :HD], queries[:, HD:])
        scores = dot(k_all[pl.ds(start, window), :], both, 1, 1)
        old = top_old[:1, :]
        top = None
        total = jnp.zeros((WORD, 2 * ROWS), f32)
        weights = []
        for t in range(window // WORD):
            there = slice(t * WORD, (t + 1) * WORD)
            keep = (words & (1 << t)) != 0
            part = scores[there, :]
            part = jnp.concatenate(
                [jnp.where(keep, part[:, :ROWS], HUGE), jnp.where(keep, part[:, ROWS:], HUGE)], 1
            )
            top = part if top is None else jnp.maximum(top, part)
            s_new[there, :] = part
            weight = jnp.exp2(s_old[there, :] * scale - old)
            total = total + weight
            weights.append(weight.astype(bf16))
        inverse = 1.0 / jnp.sum(total, axis=0, keepdims=True)
        weights = jnp.concatenate(weights, 0)
        e_ref[old_block] = weights
        there = pl.ds(old_start, ROWS)
        inv_ref[0:1, there] = inverse[:, :ROWS]
        inv_ref[1:2, there] = inverse[:, ROWS:]
        mixed = dot(vt_all[:, pl.ds(old_start, window)], weights, 1, 0) * inverse
        mixed = jnp.concatenate([mixed[:HD, :ROWS], mixed[HD:, ROWS:]], axis=0)
        mixed_ref[:, there] = mixed.astype(bf16)
        part_ref[there, :] = dot(mixed.T.astype(bf16), out_ref[...], 1, 0).astype(bf16)
        s_old[...] = s_new[...]
        top_old[...] = jnp.broadcast_to(jnp.max(top, axis=0, keepdims=True) * scale, top_old.shape)
        return carry

    lax.fori_loop(0, blocks + 1, work, 0)


def attend(places, keys, values_t, queries, w_out):
    rows = queries.shape[0]
    wide = 2 * HD
    blocks = rows // ROWS
    window = ROWS + 2 * SPAN
    shapes = [
        ((blocks, window, wide), bf16),
        ((wide, rows), bf16),
        ((8, rows), f32),
        ((rows, w_out.shape[1]), bf16),
    ]
    scratch = [
        pltpu.VMEM((3 * rows, wide), bf16),
        pltpu.VMEM((wide, 3 * rows), bf16),
        pltpu.VMEM((window, wide), f32),
        pltpu.VMEM((window, wide), f32),
        pltpu.VMEM((8, wide), f32),
    ]
    operands = (places, *keys, *values_t, queries, w_out)
    return call(forward_kernel, "attend_forward", 30.00, ATTEND_MIB, operands, shapes, scratch)


def mlp_kernel(
    head_ref, ids_ref, xm_ref, xt_ref, part_ref, other_ref, grad_ref, table_ref, up_ref, down_ref,
    middle_ref, two_ref, theirs_ref, out_ref, normed_ref, act_ref, pre_ref,
):
    head = head_ref[0]
    width = 2 * xm_ref.shape[1]
    values = ordered(head, xm_ref[...], xt_ref[...]).astype(f32)
    middle = values + (part_ref[...].astype(f32) + other_ref[...].astype(f32))
    middle_ref[...] = middle
    unit, _ = norm_rows(middle)
    level = level_values(
        ids_ref[...], jnp.concatenate([table_ref[2], table_ref[3]], axis=1)
    )
    normed = (unit * (1.0 + level[:, :width]) + level[:, width:]).astype(bf16)
    normed_ref[...] = normed
    pre = dot(normed, up_ref[...], 1, 0)
    sigma = jax.nn.sigmoid(pre)
    act = (pre * sigma).astype(bf16)
    act_ref[...] = act
    grad = grad_ref[...].astype(f32)
    grad = (grad * sigma * (1.0 + pre * (1.0 - sigma))).astype(bf16)
    pre_ref[...] = grad
    two_ref[...] = dot(grad, up_ref[...], 1, 1).astype(bf16)
    mine, theirs = parted(head, dot(act, down_ref[...], 1, 0))
    theirs_ref[...] = theirs.astype(bf16)
    out_ref[...] = parted(head, middle)[0] + mine


def mlp(head, ids, x_mine, x_theirs, part, other, grad_act, table, w_up, w_down):
    rows, half = x_mine.shape
    hidden = w_up.shape[1]
    shapes = [
        (2 * half, f32), (2 * half, bf16), (half, bf16), (half, f32),
        (2 * half, bf16), (hidden, bf16), (hidden, bf16),
    ]
    shapes = [((rows, wide), kind) for wide, kind in shapes]
    operands = (head, ids, x_mine, x_theirs, part, other, grad_act, table, w_up, w_down)
    return call(mlp_kernel, "mlp", 15.00, MLP_MIB, operands, shapes)


def branch_kernel(
    head_ref, ids_ref, middle_ref, cm_ref, ct_ref, two_ref, other_ref, mixed_ref, inv_ref, table_ref, out_ref,
    mid_ref, gout_ref, tab_ref, grad_ref, cross_ref,
):
    head = head_ref[0]
    ids = ids_ref[...]
    unit, inverse = norm_rows(middle_ref[...])
    gain = 1.0 + level_values(ids, table_ref[2])
    grad_two = two_ref[...].astype(f32) + other_ref[...].astype(f32)
    gained = grad_two * gain
    cot = ordered(head, cm_ref[...], ct_ref[...]).astype(f32)
    grad_mid = cot + inverse * (
        gained
        - jnp.mean(gained, axis=1, keepdims=True)
        - unit * jnp.mean(gained * unit, axis=1, keepdims=True)
    )
    mid_ref[...] = parted(head, grad_mid)[0]
    branch = grad_mid.astype(bf16)
    grad = dot(out_ref[...], branch, 1, 1)
    cross = grad * mixed_ref[...].astype(f32)
    for h in range(grad.shape[0] // HD):
        there = slice(h * HD, (h + 1) * HD)
        total = inv_ref[h : h + 1, :]
        grad_ref[there, :] = (grad[there, :] * total).astype(bf16)
        cross_ref[h : h + 1, :] = jnp.sum(cross[there, :], axis=0, keepdims=True) * total
    gout_ref[...] = dot(mixed_ref[...], branch, 1, 0).astype(bf16)
    tab_ref[...] = dot(
        onehot_t(ids, table_ref.shape[1]),
        jnp.concatenate(
            [parted(head, grad_two * unit)[0], parted(head, grad_two)[0]], 1
        ).astype(bf16),
        1,
        0,
    )


def branch(
    head, ids, middle, cot_mine, cot_theirs, two_part, two_other, mixed_t, inverse,
    table, w_out,
):
    rows, half = cot_mine.shape
    width = 2 * half
    shapes = [
        ((rows, half), f32),
        ((w_out.shape[0], width), bf16),
        ((table.shape[1], width), f32),
        ((2 * HD, rows), bf16),
        ((8, rows), f32),
    ]
    operands = (
        head, ids, middle, cot_mine, cot_theirs, two_part, two_other, mixed_t, inverse,
        table, w_out,
    )
    return call(branch_kernel, "branch", 6.30, BRANCH_MIB, operands, shapes)


def backward_kernel(
    e_ref, grad_ref, cross_ref, q_ref, v0, v1, v2, kt0, kt1, kt2,
    dkv_ref, dq_ref, dkv_sum, kt_all, v_all, ds_slots,
):
    blocks, window, wide = e_ref.shape
    rows = v0.shape[0]
    factor = 1.0 / math.sqrt(HD)
    dkv_sum[...] = jnp.zeros_like(dkv_sum)
    for i, (v, kt) in enumerate(((v0, kt0), (v1, kt1), (v2, kt2))):
        v_all[i * rows : (i + 1) * rows, :] = v[...]
        kt_all[:, i * rows : (i + 1) * rows] = kt[...]

    def scores_and_values(block):
        start = pl.multiple_of(block * ROWS, ROWS)
        grad = grad_ref[:, pl.ds(start, ROWS)]
        grad_both = two_blocks(grad[:HD, :], grad[HD:, :])
        cross = jnp.concatenate(
            [cross_ref[0:1, pl.ds(start, ROWS)], cross_ref[1:2, pl.ds(start, ROWS)]], axis=1
        )
        weights = e_ref[block]
        spots = pl.ds(start, window)
        grad_probs = dot(v_all[spots, :], grad_both, 1, 0)
        ds_slots[block % 2] = (weights.astype(f32) * (grad_probs - cross)).astype(bf16)
        dkv_sum[spots, wide:] += dot(weights, grad_both, 1, 1)

    def keys_and_queries(block):
        start = pl.multiple_of(block * ROWS, ROWS)
        spots = pl.ds(start, window)
        queries = q_ref[pl.ds(start, ROWS), :]
        both = two_blocks(queries[:, :HD], queries[:, HD:])
        grad_scores = ds_slots[block % 2]
        dkv_sum[spots, :wide] += dot(grad_scores, both, 1, 0)
        grad_query = dot(kt_all[:, spots], grad_scores, 1, 0) * factor
        dq_ref[pl.ds(start, ROWS), :HD] = grad_query[:HD, :ROWS].T.astype(bf16)
        dq_ref[pl.ds(start, ROWS), HD:] = grad_query[HD:, ROWS:].T.astype(bf16)

    def work(block, carry):
        scores_and_values(block)
        keys_and_queries(block - 1)
        return carry

    scores_and_values(0)
    lax.fori_loop(1, blocks, work, 0)
    keys_and_queries(blocks - 1)
    for i in range(3):
        there = slice(i * rows, (i + 1) * rows)
        dkv_ref[there, :wide] = (dkv_sum[there, :wide] * factor).astype(bf16)
        dkv_ref[there, wide:] = dkv_sum[there, wide:].astype(bf16)


def backward(weights, grad_t, cross, queries, values, keys_t):
    rows = queries.shape[0]
    wide = 2 * HD
    window = weights.shape[1]
    shapes = [((3 * rows, 2 * wide), bf16), ((rows, wide), bf16)]
    scratch = [
        pltpu.VMEM((3 * rows, 2 * wide), f32),
        pltpu.VMEM((wide, 3 * rows), bf16),
        pltpu.VMEM((3 * rows, wide), bf16),
        pltpu.VMEM((2, window, wide), bf16),
    ]
    operands = (weights, grad_t, cross, queries, *values, *keys_t)
    return call(backward_kernel, "attend_backward", 25.20, BACK_MIB, operands, shapes, scratch)


def grads_kernel(
    head_ref, dkv_ref, dq_ref, id0, id1, id2, n0, n1, n2, u0, u1, u2, key_ref, value_ref, query_ref,
    gq_ref, gkv_ref, mine_ref, theirs_ref, tab_mine, tab_theirs,
):
    head = head_ref[0]
    rows, width = n0.shape
    wide = dq_ref.shape[1]
    levels = tab_mine.shape[0]
    w_kv = jnp.concatenate([key_ref[...], value_ref[...]], axis=1)
    grad_kv = jnp.zeros((width, 2 * wide), f32)
    table_sum = jnp.zeros((levels, 2 * width), f32)
    for i, (ids, normed, units) in enumerate(((id0, n0, u0), (id1, n1, u1), (id2, n2, u2))):
        there = slice(i * rows, (i + 1) * rows)
        dkv = dkv_ref[there, :]
        grad_kv = grad_kv + dot(normed[...], dkv, 0, 0)
        part = dot(dkv, w_kv, 1, 1)
        if i == 1:
            part = part + dot(dq_ref[...], query_ref[...], 1, 1)
        mine, theirs = parted(head, part)
        mine_ref[there, :] = mine.astype(bf16)
        theirs_ref[there, :] = theirs.astype(bf16)
        table_sum = table_sum + dot(
            onehot_t(ids[...], levels),
            jnp.concatenate([part * units[...].astype(f32), part], 1).astype(bf16),
            1,
            0,
        )
    gkv_ref[...] = grad_kv.astype(bf16)
    gq_ref[...] = dot(n1[...], dq_ref[...], 0, 0).astype(bf16)
    scale_mine, scale_theirs = parted(head, table_sum[:, :width])
    shift_mine, shift_theirs = parted(head, table_sum[:, width:])
    tab_mine[...] = jnp.concatenate([scale_mine, shift_mine], axis=1)
    tab_theirs[...] = jnp.concatenate([scale_theirs, shift_theirs], axis=1)


def grads(head, dkv, dq, ids, normed, units, w_key, w_value, w_query, levels):
    rows, width = normed[0].shape
    half = width // 2
    wide = dq.shape[1]
    shapes = [
        ((width, wide), bf16),
        ((width, 2 * wide), bf16),
        ((3 * rows, half), bf16),
        ((3 * rows, half), bf16),
        ((levels, width), f32),
        ((levels, width), f32),
    ]
    operands = (head, dkv, dq, *ids, *normed, *units, w_key, w_value, w_query)
    return call(grads_kernel, "grads", 10.50, GRADS_MIB, operands, shapes)


def unpack_mlp_kernel(x_ref, y_ref, a, a_near, a_far, b, b_near, b_far, up_ref, down_ref):
    x, y = x_ref[0], y_ref[0]
    count, width = a.shape

    def put_up(ref, start, at_x, at_y):
        spots = pl.ds(pl.multiple_of(at_y * count, count), count)
        lanes = pl.ds(pl.multiple_of(at_x * width, width), width)
        up_ref[spots, lanes] = ref[start : start + count, :].astype(f32)

    def put_down(ref, start, at_x, at_y):
        spots = pl.ds(pl.multiple_of((2 * at_y + at_x) * count, count), count)
        down_ref[spots, :] = ref[start : start + count, :].astype(f32)

    put_up(a, 0, x, y)
    put_up(a_near, 0, x, 1 - y)
    put_up(a_far, 0, 1 - x, y)
    put_up(a_far, count, 1 - x, 1 - y)
    put_down(b, 0, x, y)
    put_down(b_near, 0, 1 - x, y)
    put_down(b_far, 0, x, 1 - y)
    put_down(b_far, count, 1 - x, 1 - y)


def unpack_mlp(x, y, *pieces):
    count, width = pieces[0].shape
    shapes = [((2 * count, 2 * width), f32), ((4 * count, width), f32)]
    return call(unpack_mlp_kernel, "unpack_mlp", 4.50, UNPACK_MIB, (x, y, *pieces), shapes)


def unpack_kernel(
    x_ref, y_ref, c, c_near, c_far, d, d_near, d_far, tab,
    q_ref, k_ref, v_ref, out_ref, tab_ref, first, second,
):
    x, y = x_ref[0], y_ref[0]
    count = d.shape[0]

    def put(total, ref, start, low, high):
        spots = pl.ds(pl.multiple_of((2 * low + high) * count, count), count)
        total[spots, :] = ref[start : start + count, :].astype(f32)

    put(first, c, 0, x, y)
    put(first, c_near, 0, x, 1 - y)
    put(first, c_far, 0, 1 - x, y)
    put(first, c_far, count, 1 - x, 1 - y)
    put(second, d, 0, y, x)
    put(second, d_near, 0, y, 1 - x)
    put(second, d_far, 0, 1 - y, x)
    put(second, d_far, count, 1 - y, 1 - x)
    wide = q_ref.shape[1]
    out_rows = out_ref.shape[0]
    levels = tab_ref.shape[1]
    q_ref[...] = first[:, :wide]
    k_ref[...] = first[:, wide:]
    v_ref[...] = second[:, :wide]
    out_ref[:, :wide] = second[:out_rows, wide:]
    out_ref[:, wide:] = second[out_rows:, wide:]
    table = tab[...] + c_far[2 * count :, :].astype(f32)
    tab_ref[0] = table[:levels, :wide]
    tab_ref[1] = table[:levels, wide:]
    tab_ref[2] = table[levels:, :wide]
    tab_ref[3] = table[levels:, wide:]


def unpack(x, y, c, c_near, c_far, d, d_near, d_far, tab, wide, rows):
    count, width = d.shape
    depth = 4 * count
    shapes = [((depth, wide), f32)] * 3
    shapes += [((rows, width), f32), ((4, tab.shape[0] // 2, wide), f32)]
    scratch = [pltpu.VMEM((depth, width), f32)] * 2
    operands = (x, y, c, c_near, c_far, d, d_near, d_far, tab)
    return call(unpack_kernel, "unpack", 4.50, UNPACK_MIB, operands, shapes, scratch)


def passed_along(block, axis, distance):
    devices = range(lax.axis_size(axis))
    route = [((i - distance) % len(devices), i) for i in devices]
    return lax.ppermute(block, axis, route)


def swapped(block, axis, bit):
    devices = range(lax.axis_size(axis))
    return lax.ppermute(block, axis, [(i, i ^ bit) for i in devices])


def together(*blocks):
    return lax.optimization_barrier(blocks)


def held_until(block, *others):
    return lax.optimization_barrier((block, *others))[0]


def two_parts(block, axis, bit):
    half = block.shape[0] // 2
    upper = (lax.axis_index(axis) & bit) != 0
    send = jnp.where(upper, block[:half], block[half:])
    keep = jnp.where(upper, block[half:], block[:half])
    return send, keep


def added(keep, got):
    return (keep.astype(f32) + got.astype(f32)).astype(bf16)


def picked(pieces, place, j):
    return jnp.where(
        place == 0,
        pieces[j],
        jnp.where(
            place == 1, pieces[1 ^ j], jnp.where(place == 2, pieces[2 ^ j], pieces[3 ^ j])
        ),
    )


def quarters(block, place):
    count = block.shape[0] // 4
    pieces = [block[i * count : (i + 1) * count] for i in range(4)]
    return [picked(pieces, place, j) for j in range(4)]


def to_others(pieces, axis, bit):
    return [swapped(piece, axis, (j + 1) * bit) for j, piece in enumerate(pieces)]


def total(pieces):
    result = pieces[0].astype(f32)
    for piece in pieces[1:]:
        result = result + piece.astype(f32)
    return result


def sum_further(block, axis):
    size = lax.axis_size(axis)
    if size > 16:
        groups = [[j * 16 + i for j in range(size // 16)] for i in range(16)]
        block = lax.psum(block, axis, axis_index_groups=groups)
    return block


def body(
    inputs,
    w_query,
    w_key,
    w_value,
    w_out,
    w_up,
    w_down,
    mod_table,
    level_ids,
    neighbours,
    cotangent,
):
    rows, half = inputs.shape
    width = half * lax.axis_size("heads")
    levels = mod_table.shape[1]
    head = lax.axis_index("heads").astype(jnp.int32).reshape(1)
    first_head = lax.axis_index("heads") == 0
    ids_own = level_ids[None, :]

    before = passed_along(inputs, "nodes", 1)
    after = passed_along(inputs, "nodes", -1)
    in_other = swapped(inputs, "heads", 1)
    cot_other = swapped(cotangent, "heads", 1)
    own = front(head, ids_own, inputs, in_other, mod_table, w_key, w_value, w_query)
    queries, keys_t1, values1 = own[4:]
    ids_late = held_until(ids_own, own[0])
    ids_before = passed_along(ids_late, "nodes", 1)
    ids_after = passed_along(ids_late, "nodes", -1)
    node_count = rows * lax.axis_size("nodes")
    first_node = lax.axis_index("nodes") * rows
    places = jnp.mod(neighbours.T - first_node + SPAN, node_count)
    full_cot = jnp.where(
        first_head,
        jnp.concatenate([cotangent, cot_other], axis=1),
        jnp.concatenate([cot_other, cotangent], axis=1),
    )
    grad_act = dot(full_cot, w_down, 1, 1).astype(bf16)
    before_other = swapped(held_until(before, own[0], grad_act, ids_before, ids_after), "heads", 1)
    low = front(head, ids_before, before, before_other, mod_table, w_key, w_value)
    after_other = swapped(after, "heads", 1)
    high = front(head, ids_after, after, after_other, mod_table, w_key, w_value)
    normed, units, keys, values_t = zip(low, own[:4], high)
    weights, mixed_t, inverse, attn_part = attend(places, keys, values_t, queries, w_out)
    attn_other = swapped(attn_part, "heads", 1)
    middle, two_part, mlp_theirs, out_mine, normed_two, activated, grad_pre = mlp(
        head, ids_own, inputs, in_other, attn_part, attn_other, grad_act, mod_table, w_up, w_down
    )
    two_other = swapped(two_part, "heads", 1)
    grad_up = dot(normed_two, grad_pre, 0, 0).astype(bf16)
    grad_down = dot(activated, full_cot, 0, 0).astype(bf16)
    hidden = grad_up.shape[1] // 2
    grad_up = jnp.concatenate([grad_up[:, :hidden], grad_up[:, hidden:]])
    up_send, up_keep = two_parts(grad_up, "nodes", 1)
    down_send, down_keep = two_parts(grad_down, "nodes", 2)
    place = lax.axis_index("nodes").astype(jnp.int32).reshape(1)
    x, y, z_low, z_high = [jnp.bitwise_and(jnp.right_shift(place, bit), 1) for bit in range(4)]
    up_got = swapped(up_send, "nodes", 1)
    down_got = swapped(down_send, "nodes", 2)
    mlp_other = swapped(mlp_theirs, "heads", 1)
    output = (out_mine + mlp_other.astype(f32)).astype(bf16)

    keys_t = [
        dot(w_key, normed[0], 0, 1).astype(bf16),
        keys_t1,
        dot(w_key, normed[2], 0, 1).astype(bf16),
    ]
    values = [
        dot(normed[0], w_value, 1, 0).astype(bf16),
        values1,
        dot(normed[2], w_value, 1, 0).astype(bf16),
    ]
    mid_mine, grad_out, tab_two, grad_t, cross = branch(
        head, ids_own, middle, cotangent, cot_other, two_part, two_other, mixed_t, inverse,
        mod_table, w_out,
    )
    grad_t = held_until(grad_t, up_send, down_send)
    dkv, dq = backward(weights, grad_t, cross, queries, values, keys_t)
    up_send, up_keep = two_parts(added(up_keep, held_until(up_got, dq)), "nodes", 2)
    down_send, down_keep = two_parts(added(down_keep, held_until(down_got, dq)), "nodes", 1)
    up_got = swapped(up_send, "nodes", 2)
    down_got = swapped(down_send, "nodes", 1)
    dq = held_until(dq, up_send, down_send)
    grad_q, grad_kv, one_mine, one_theirs, tab_mine, tab_theirs = grads(
        head, dkv, dq, (ids_before, ids_own, ids_after), normed, units,
        w_key, w_value, w_query, levels,
    )
    one_other = swapped(one_theirs, "heads", 1)
    tab_other = swapped(tab_theirs, "heads", 1)
    up_got, down_got = held_until((up_got, down_got), grad_q)
    grad_q, grad_kv, grad_out = sum_further((grad_q, grad_kv, grad_out), "nodes")
    wide = grad_q.shape[1]
    spot = jnp.bitwise_and(jnp.right_shift(lax.axis_index("nodes"), 2), 3)
    m = jnp.concatenate([added(up_keep, up_got), added(down_keep, down_got)])
    m_parts = quarters(m, spot)
    c = jnp.concatenate([grad_q, grad_kv[:, :wide]], axis=1)
    d = jnp.concatenate([grad_out[:, :wide], grad_out[:, wide:]], axis=0)
    d = jnp.concatenate([grad_kv[:, wide:], d], axis=1)
    c_send, c_keep = two_parts(c, "nodes", 1)
    d_send, d_keep = two_parts(d, "nodes", 2)
    c_send, d_send, *m_parts = together(c_send, d_send, *m_parts)
    c_got, d_got, tab_other, one_other, *m_got = together(
        swapped(c_send, "nodes", 1),
        swapped(d_send, "nodes", 2),
        tab_other,
        one_other,
        *to_others(m_parts[1:], "nodes", 4),
    )
    c_send, c_keep = two_parts(added(c_keep, c_got), "nodes", 2)
    d_send, d_keep = two_parts(added(d_keep, d_got), "nodes", 1)
    m = sum_further(total([m_parts[0], *m_got]).astype(bf16), "nodes")
    one_all = one_mine.astype(f32) + one_other.astype(f32)
    to_before, to_after = one_all[:rows].astype(bf16), one_all[2 * rows :].astype(bf16)
    c_send, d_send, m, to_before, to_after = together(c_send, d_send, m, to_before, to_after)
    to_before = passed_along(to_before, "nodes", -1)
    to_after = passed_along(to_after, "nodes", 1)
    c_got, d_got, *m_got = together(
        swapped(c_send, "nodes", 2),
        swapped(d_send, "nodes", 1),
        *to_others([m] * 3, "nodes", 4),
    )
    m_parts = [picked([m, *m_got], spot, i) for i in range(4)]
    a, b = jnp.concatenate(m_parts[:2]), jnp.concatenate(m_parts[2:])
    table = sum_further(jnp.concatenate([tab_mine + tab_other, tab_two], axis=0), "nodes")
    cd = jnp.concatenate(
        [total([c_keep, c_got]), total([d_keep, d_got]), table], axis=0
    ).astype(bf16)
    a, b, *cd_parts = together(a, b, *quarters(cd, spot))
    cd_got = together(*to_others(cd_parts[1:], "nodes", 4))
    cd = total([cd_parts[0], *cd_got]).astype(bf16)
    a, b, cd, to_before, to_after = together(a, b, cd, to_before, to_after)
    a_near, b_near, *cd_got = together(
        swapped(a, "nodes", 2),
        swapped(b, "nodes", 1),
        *to_others([cd] * 3, "nodes", 4),
    )
    cd = jnp.concatenate([picked([cd, *cd_got], spot, i) for i in range(4)])
    count = cd.shape[0] // 2 - levels
    a_send, b_send, c, d = together(
        jnp.concatenate([a, a_near]),
        jnp.concatenate([b, b_near]),
        jnp.concatenate([cd[:count], cd[2 * count :]]),
        cd[count : 2 * count],
    )
    grad_one = one_all[rows : 2 * rows] + to_before.astype(f32) + to_after.astype(f32)
    full_in = jnp.concatenate([inputs, in_other], axis=1).astype(f32)
    unit, inverse = norm_rows(full_in)
    unit = unit[:, :half]
    onehot = (level_ids[:, None] == jnp.arange(levels, dtype=jnp.int32)[None, :]).astype(f32)
    scale_mine = jnp.where(first_head, mod_table[0][:, :half], mod_table[0][:, half:])
    gain = 1.0 + jnp.dot(onehot, scale_mine, precision=lax.Precision.HIGHEST)
    gained = grad_one * gain
    sum_gain, sum_cross = lax.psum(
        (jnp.sum(gained, axis=1), jnp.sum(gained * unit, axis=1)), "heads"
    )
    grad_inputs = mid_mine + inverse * (
        gained - sum_gain[:, None] / width - unit * sum_cross[:, None] / width
    )
    a_far, b_far, c_near, d_near, grad_inputs = together(
        swapped(a_send, "nodes", 1),
        swapped(b_send, "nodes", 2),
        swapped(c, "nodes", 2),
        swapped(d, "nodes", 1),
        grad_inputs,
    )
    tab = total([c[count:], c_near[count:]])
    c_send = jnp.concatenate([c[:count], c_near[:count], tab.astype(bf16)])
    c_far = swapped(c_send, "nodes", 1)
    d_far = swapped(jnp.concatenate([d, d_near]), "nodes", 2)
    up_total, down_total = unpack_mlp(x, y, a, a_near, a_far, b, b_near, b_far)
    c_far, d_far = held_until((c_far, d_far), up_total)
    query_total, key_total, value_total, out_total, table_total = unpack(
        x, y, c, c_near, c_far, d, d_near, d_far, tab, wide, grad_out.shape[0]
    )
    return (
        output,
        grad_inputs,
        query_total,
        key_total,
        value_total,
        out_total,
        up_total,
        down_total,
        table_total,
    )


def solution(mesh):
    return jax.shard_map(
        body,
        mesh=mesh,
        in_specs=(
            P("nodes", "heads"),
            P(None, "heads"),
            P(None, "heads"),
            P(None, "heads"),
            P("heads", None),
            P(None, "heads"),
            P("heads", None),
            P(),
            P("nodes"),
            P("nodes", None),
            P("nodes", "heads"),
        ),
        out_specs=(
            P("nodes", "heads"),
            P("nodes", "heads"),
            P(None, "heads"),
            P(None, "heads"),
            P(None, "heads"),
            P("heads", None),
            P(None, "heads"),
            P("heads", None),
            P(None, None, "heads"),
        ),
        check_vma=False,
    )
```

```python
import math

import jax
import jax.numpy as jnp
from jax import lax
from jax.experimental import pallas as pl
from jax.experimental.pallas import tpu as pltpu
from jax.sharding import PartitionSpec as P

HD = 128
K = 16
SPAN = 896
ROWS = 128
WORD = 64
HUGE = -1e30
MIB = 1024 * 1024
FRONT_MIB = 20
ATTEND_MIB = 20
MLP_MIB = 24
BRANCH_MIB = 14
BACK_MIB = 32
GRADS_MIB = 20
UNPACK_MIB = 8
epsilon = 1e-05
bf16 = jnp.bfloat16
f32 = jnp.float32


def dot(left, right, left_dim, right_dim):
    return lax.dot_general(
        left,
        right,
        (((left_dim,), (right_dim,)), ((), ())),
        preferred_element_type=f32,
    )


def two_blocks(first, second):
    zero = jnp.zeros_like(first)
    return jnp.concatenate(
        [jnp.concatenate([first, zero], 1), jnp.concatenate([zero, second], 1)], 0
    )


def ordered(head, mine, theirs):
    return jnp.where(
        head == 0,
        jnp.concatenate([mine, theirs], axis=1),
        jnp.concatenate([theirs, mine], axis=1),
    )


def parted(head, block):
    half = block.shape[1] // 2
    low, high = block[:, :half], block[:, half:]
    return jnp.where(head == 0, low, high), jnp.where(head == 0, high, low)


def onehot_t(ids, levels):
    spots = lax.broadcasted_iota(jnp.int32, (levels, ids.shape[1]), 0)
    return jnp.where(spots == ids, 1.0, 0.0).astype(bf16)


def level_values(ids, table):
    chosen = onehot_t(ids, table.shape[0])
    first = table.astype(bf16)
    rest = table - first.astype(f32)
    second = rest.astype(bf16)
    third = (rest - second.astype(f32)).astype(bf16)
    return dot(
        jnp.concatenate([chosen] * 3, axis=0),
        jnp.concatenate([first, second, third], axis=0),
        0,
        0,
    )


def norm_rows(values):
    centred = values - jnp.mean(values, axis=1, keepdims=True)
    inverse = lax.rsqrt(jnp.mean(centred * centred, axis=1, keepdims=True) + epsilon)
    return centred * inverse, inverse


def cost(microseconds):
    return pl.CostEstimate(
        flops=int(microseconds * 5e8), bytes_accessed=int(microseconds * 2.5e6), transcendentals=0
    )


def call(kernel, name, microseconds, mebibytes, operands, out_shape, scratch=()):
    spaces = [
        pltpu.SMEM if operand.shape == (1,) else pltpu.VMEM for operand in operands
    ]
    return pl.pallas_call(
        kernel,
        in_specs=[pl.BlockSpec(memory_space=space) for space in spaces],
        out_shape=[jax.ShapeDtypeStruct(shape, kind) for shape, kind in out_shape],
        scratch_shapes=list(scratch),
        compiler_params=pltpu.CompilerParams(vmem_limit_bytes=mebibytes * MIB),
        cost_estimate=cost(microseconds),
        name=name,
    )(*operands)


def front_kernel(
    head_ref, ids_ref, mine_ref, theirs_ref, table_ref, key_ref, value_ref, *refs
):
    width = 2 * mine_ref.shape[1]
    more = len(refs) > 4
    normed_ref, unit_ref, k_ref, vt_ref = refs[-4:] if not more else refs[1:5]
    values = ordered(head_ref[0], mine_ref[...], theirs_ref[...]).astype(f32)
    unit, _ = norm_rows(values)
    level = level_values(
        ids_ref[...], jnp.concatenate([table_ref[0], table_ref[1]], axis=1)
    )
    normed = (unit * (1.0 + level[:, :width]) + level[:, width:]).astype(bf16)
    normed_ref[...] = normed
    unit_ref[...] = unit.astype(bf16)
    k_ref[...] = dot(normed, key_ref[...], 1, 0).astype(bf16)
    vt_ref[...] = dot(value_ref[...], normed, 0, 1).astype(bf16)
    if more:
        query_ref, (q_ref, kt_ref, v_ref) = refs[0], refs[5:]
        q_ref[...] = dot(normed, query_ref[...], 1, 0).astype(bf16)
        kt_ref[...] = dot(key_ref[...], normed, 0, 1).astype(bf16)
        v_ref[...] = dot(normed, value_ref[...], 1, 0).astype(bf16)


def front(head, ids, mine, theirs, table, w_key, w_value, *w_query):
    rows = mine.shape[0]
    width = 2 * mine.shape[1]
    wide = 2 * HD
    down, along = ((rows, wide), bf16), ((wide, rows), bf16)
    shapes = [((rows, width), bf16)] * 2 + [down, along]
    if w_query:
        shapes += [down, along, down]
    operands = (head, ids, mine, theirs, table, w_key, w_value, *w_query)
    return call(front_kernel, "front", 10.50, FRONT_MIB, operands, shapes)


def forward_kernel(
    nbr_ref, k0, k1, k2, vt0, vt1, vt2, q_ref, out_ref,
    e_ref, mixed_ref, inv_ref, part_ref, k_all, vt_all, s_new, s_old, top_old,
):
    blocks, window, _ = e_ref.shape
    rows = k0.shape[0]
    scale = math.log2(math.e) / math.sqrt(HD)
    for i, (k, vt) in enumerate(((k0, vt0), (k1, vt1), (k2, vt2))):
        k_all[i * rows : (i + 1) * rows, :] = k[...]
        vt_all[:, i * rows : (i + 1) * rows] = vt[...]
    s_old[...] = jnp.zeros_like(s_old)
    top_old[...] = jnp.zeros_like(top_old)

    def work(step, carry):
        old_block = jnp.maximum(step - 1, 0)
        start = pl.multiple_of(jnp.minimum(step, blocks - 1) * ROWS, ROWS)
        old_start = pl.multiple_of(old_block * ROWS, ROWS)
        place = nbr_ref[:, pl.ds(start, ROWS)] - start
        bit = jnp.left_shift(1, jnp.right_shift(place, 6))
        low = jnp.bitwise_and(place, WORD - 1)
        lane_low = lax.broadcasted_iota(jnp.int32, (WORD, ROWS), 0)
        words = jnp.zeros((WORD, ROWS), jnp.int32)
        for j in range(K):
            words = words | jnp.where(lane_low == low[j : j + 1, :], bit[j : j + 1, :], 0)
        queries = q_ref[pl.ds(start, ROWS), :]
        both = two_blocks(queries[:, :HD], queries[:, HD:])
        scores = dot(k_all[pl.ds(start, window), :], both, 1, 1)
        old = top_old[:1, :]
        top = None
        total = jnp.zeros((WORD, 2 * ROWS), f32)
        weights = []
        for t in range(window // WORD):
            there = slice(t * WORD, (t + 1) * WORD)
            keep = (words & (1 << t)) != 0
            part = scores[there, :]
            part = jnp.concatenate(
                [jnp.where(keep, part[:, :ROWS], HUGE), jnp.where(keep, part[:, ROWS:], HUGE)], 1
            )
            top = part if top is None else jnp.maximum(top, part)
            s_new[there, :] = part
            weight = jnp.exp2(s_old[there, :] * scale - old)
            total = total + weight
            weights.append(weight.astype(bf16))
        inverse = 1.0 / jnp.sum(total, axis=0, keepdims=True)
        weights = jnp.concatenate(weights, 0)
        e_ref[old_block] = weights
        there = pl.ds(old_start, ROWS)
        inv_ref[0:1, there] = inverse[:, :ROWS]
        inv_ref[1:2, there] = inverse[:, ROWS:]
        mixed = dot(vt_all[:, pl.ds(old_start, window)], weights, 1, 0) * inverse
        mixed = jnp.concatenate([mixed[:HD, :ROWS], mixed[HD:, ROWS:]], axis=0)
        mixed_ref[:, there] = mixed.astype(bf16)
        part_ref[there, :] = dot(mixed.T.astype(bf16), out_ref[...], 1, 0).astype(bf16)
        s_old[...] = s_new[...]
        top_old[...] = jnp.broadcast_to(jnp.max(top, axis=0, keepdims=True) * scale, top_old.shape)
        return carry

    lax.fori_loop(0, blocks + 1, work, 0)


def attend(places, keys, values_t, queries, w_out):
    rows = queries.shape[0]
    wide = 2 * HD
    blocks = rows // ROWS
    window = ROWS + 2 * SPAN
    shapes = [
        ((blocks, window, wide), bf16),
        ((wide, rows), bf16),
        ((8, rows), f32),
        ((rows, w_out.shape[1]), bf16),
    ]
    scratch = [
        pltpu.VMEM((3 * rows, wide), bf16),
        pltpu.VMEM((wide, 3 * rows), bf16),
        pltpu.VMEM((window, wide), f32),
        pltpu.VMEM((window, wide), f32),
        pltpu.VMEM((8, wide), f32),
    ]
    operands = (places, *keys, *values_t, queries, w_out)
    return call(forward_kernel, "attend_forward", 35.00, ATTEND_MIB, operands, shapes, scratch)


def mlp_kernel(
    head_ref, ids_ref, xm_ref, xt_ref, part_ref, other_ref, grad_ref, table_ref, up_ref, down_ref,
    middle_ref, two_ref, theirs_ref, out_ref, normed_ref, act_ref, pre_ref,
):
    head = head_ref[0]
    width = 2 * xm_ref.shape[1]
    values = ordered(head, xm_ref[...], xt_ref[...]).astype(f32)
    middle = values + (part_ref[...].astype(f32) + other_ref[...].astype(f32))
    middle_ref[...] = middle
    unit, _ = norm_rows(middle)
    level = level_values(
        ids_ref[...], jnp.concatenate([table_ref[2], table_ref[3]], axis=1)
    )
    normed = (unit * (1.0 + level[:, :width]) + level[:, width:]).astype(bf16)
    normed_ref[...] = normed
    pre = dot(normed, up_ref[...], 1, 0)
    sigma = jax.nn.sigmoid(pre)
    act = (pre * sigma).astype(bf16)
    act_ref[...] = act
    grad = grad_ref[...].astype(f32)
    grad = (grad * sigma * (1.0 + pre * (1.0 - sigma))).astype(bf16)
    pre_ref[...] = grad
    two_ref[...] = dot(grad, up_ref[...], 1, 1).astype(bf16)
    mine, theirs = parted(head, dot(act, down_ref[...], 1, 0))
    theirs_ref[...] = theirs.astype(bf16)
    out_ref[...] = parted(head, middle)[0] + mine


def mlp(head, ids, x_mine, x_theirs, part, other, grad_act, table, w_up, w_down):
    rows, half = x_mine.shape
    hidden = w_up.shape[1]
    shapes = [
        (2 * half, f32), (2 * half, bf16), (half, bf16), (half, f32),
        (2 * half, bf16), (hidden, bf16), (hidden, bf16),
    ]
    shapes = [((rows, wide), kind) for wide, kind in shapes]
    operands = (head, ids, x_mine, x_theirs, part, other, grad_act, table, w_up, w_down)
    return call(mlp_kernel, "mlp", 10.50, MLP_MIB, operands, shapes)


def branch_kernel(
    head_ref, ids_ref, middle_ref, cm_ref, ct_ref, two_ref, other_ref, mixed_ref, inv_ref, table_ref, out_ref,
    mid_ref, gout_ref, tab_ref, grad_ref, cross_ref,
):
    head = head_ref[0]
    ids = ids_ref[...]
    unit, inverse = norm_rows(middle_ref[...])
    gain = 1.0 + level_values(ids, table_ref[2])
    grad_two = two_ref[...].astype(f32) + other_ref[...].astype(f32)
    gained = grad_two * gain
    cot = ordered(head, cm_ref[...], ct_ref[...]).astype(f32)
    grad_mid = cot + inverse * (
        gained
        - jnp.mean(gained, axis=1, keepdims=True)
        - unit * jnp.mean(gained * unit, axis=1, keepdims=True)
    )
    mid_ref[...] = parted(head, grad_mid)[0]
    branch = grad_mid.astype(bf16)
    grad = dot(out_ref[...], branch, 1, 1)
    cross = grad * mixed_ref[...].astype(f32)
    for h in range(grad.shape[0] // HD):
        there = slice(h * HD, (h + 1) * HD)
        total = inv_ref[h : h + 1, :]
        grad_ref[there, :] = (grad[there, :] * total).astype(bf16)
        cross_ref[h : h + 1, :] = jnp.sum(cross[there, :], axis=0, keepdims=True) * total
    gout_ref[...] = dot(mixed_ref[...], branch, 1, 0).astype(bf16)
    tab_ref[...] = dot(
        onehot_t(ids, table_ref.shape[1]),
        jnp.concatenate(
            [parted(head, grad_two * unit)[0], parted(head, grad_two)[0]], 1
        ).astype(bf16),
        1,
        0,
    )


def branch(
    head, ids, middle, cot_mine, cot_theirs, two_part, two_other, mixed_t, inverse,
    table, w_out,
):
    rows, half = cot_mine.shape
    width = 2 * half
    shapes = [
        ((rows, half), f32),
        ((w_out.shape[0], width), bf16),
        ((table.shape[1], width), f32),
        ((2 * HD, rows), bf16),
        ((8, rows), f32),
    ]
    operands = (
        head, ids, middle, cot_mine, cot_theirs, two_part, two_other, mixed_t, inverse,
        table, w_out,
    )
    return call(branch_kernel, "branch", 6.30, BRANCH_MIB, operands, shapes)


def backward_kernel(
    e_ref, grad_ref, cross_ref, q_ref, v0, v1, v2, kt0, kt1, kt2,
    dkv_ref, dq_ref, dkv_sum, kt_all, v_all, ds_slots,
):
    blocks, window, wide = e_ref.shape
    rows = v0.shape[0]
    factor = 1.0 / math.sqrt(HD)
    dkv_sum[...] = jnp.zeros_like(dkv_sum)
    for i, (v, kt) in enumerate(((v0, kt0), (v1, kt1), (v2, kt2))):
        v_all[i * rows : (i + 1) * rows, :] = v[...]
        kt_all[:, i * rows : (i + 1) * rows] = kt[...]

    def scores_and_values(block):
        start = pl.multiple_of(block * ROWS, ROWS)
        grad = grad_ref[:, pl.ds(start, ROWS)]
        grad_both = two_blocks(grad[:HD, :], grad[HD:, :])
        cross = jnp.concatenate(
            [cross_ref[0:1, pl.ds(start, ROWS)], cross_ref[1:2, pl.ds(start, ROWS)]], axis=1
        )
        weights = e_ref[block]
        spots = pl.ds(start, window)
        grad_probs = dot(v_all[spots, :], grad_both, 1, 0)
        ds_slots[block % 2] = (weights.astype(f32) * (grad_probs - cross)).astype(bf16)
        dkv_sum[spots, wide:] += dot(weights, grad_both, 1, 1)

    def keys_and_queries(block):
        start = pl.multiple_of(block * ROWS, ROWS)
        spots = pl.ds(start, window)
        queries = q_ref[pl.ds(start, ROWS), :]
        both = two_blocks(queries[:, :HD], queries[:, HD:])
        grad_scores = ds_slots[block % 2]
        dkv_sum[spots, :wide] += dot(grad_scores, both, 1, 0)
        grad_query = dot(kt_all[:, spots], grad_scores, 1, 0) * factor
        dq_ref[pl.ds(start, ROWS), :HD] = grad_query[:HD, :ROWS].T.astype(bf16)
        dq_ref[pl.ds(start, ROWS), HD:] = grad_query[HD:, ROWS:].T.astype(bf16)

    def work(block, carry):
        scores_and_values(block)
        keys_and_queries(block - 1)
        return carry

    scores_and_values(0)
    lax.fori_loop(1, blocks, work, 0)
    keys_and_queries(blocks - 1)
    for i in range(3):
        there = slice(i * rows, (i + 1) * rows)
        dkv_ref[there, :wide] = (dkv_sum[there, :wide] * factor).astype(bf16)
        dkv_ref[there, wide:] = dkv_sum[there, wide:].astype(bf16)


def backward(weights, grad_t, cross, queries, values, keys_t):
    rows = queries.shape[0]
    wide = 2 * HD
    window = weights.shape[1]
    shapes = [((3 * rows, 2 * wide), bf16), ((rows, wide), bf16)]
    scratch = [
        pltpu.VMEM((3 * rows, 2 * wide), f32),
        pltpu.VMEM((wide, 3 * rows), bf16),
        pltpu.VMEM((3 * rows, wide), bf16),
        pltpu.VMEM((2, window, wide), bf16),
    ]
    operands = (weights, grad_t, cross, queries, *values, *keys_t)
    return call(backward_kernel, "attend_backward", 67.20, BACK_MIB, operands, shapes, scratch)


def grads_kernel(
    head_ref, dkv_ref, dq_ref, id0, id1, id2, n0, n1, n2, u0, u1, u2, key_ref, value_ref, query_ref,
    gq_ref, gkv_ref, mine_ref, theirs_ref, tab_mine, tab_theirs,
):
    head = head_ref[0]
    rows, width = n0.shape
    wide = dq_ref.shape[1]
    levels = tab_mine.shape[0]
    w_kv = jnp.concatenate([key_ref[...], value_ref[...]], axis=1)
    grad_kv = jnp.zeros((width, 2 * wide), f32)
    table_sum = jnp.zeros((levels, 2 * width), f32)
    for i, (ids, normed, units) in enumerate(((id0, n0, u0), (id1, n1, u1), (id2, n2, u2))):
        there = slice(i * rows, (i + 1) * rows)
        dkv = dkv_ref[there, :]
        grad_kv = grad_kv + dot(normed[...], dkv, 0, 0)
        part = dot(dkv, w_kv, 1, 1)
        if i == 1:
            part = part + dot(dq_ref[...], query_ref[...], 1, 1)
        mine, theirs = parted(head, part)
        mine_ref[there, :] = mine.astype(bf16)
        theirs_ref[there, :] = theirs.astype(bf16)
        table_sum = table_sum + dot(
            onehot_t(ids[...], levels),
            jnp.concatenate([part * units[...].astype(f32), part], 1).astype(bf16),
            1,
            0,
        )
    gkv_ref[...] = grad_kv.astype(bf16)
    gq_ref[...] = dot(n1[...], dq_ref[...], 0, 0).astype(bf16)
    scale_mine, scale_theirs = parted(head, table_sum[:, :width])
    shift_mine, shift_theirs = parted(head, table_sum[:, width:])
    tab_mine[...] = jnp.concatenate([scale_mine, shift_mine], axis=1)
    tab_theirs[...] = jnp.concatenate([scale_theirs, shift_theirs], axis=1)


def grads(head, dkv, dq, ids, normed, units, w_key, w_value, w_query, levels):
    rows, width = normed[0].shape
    half = width // 2
    wide = dq.shape[1]
    shapes = [
        ((width, wide), bf16),
        ((width, 2 * wide), bf16),
        ((3 * rows, half), bf16),
        ((3 * rows, half), bf16),
        ((levels, width), f32),
        ((levels, width), f32),
    ]
    operands = (head, dkv, dq, *ids, *normed, *units, w_key, w_value, w_query)
    return call(grads_kernel, "grads", 17.50, GRADS_MIB, operands, shapes)


def unpack_mlp_kernel(x_ref, y_ref, a, a_near, a_far, b, b_near, b_far, up_ref, down_ref):
    x, y = x_ref[0], y_ref[0]
    count, width = a.shape

    def put_up(ref, start, at_x, at_y):
        spots = pl.ds(pl.multiple_of(at_y * count, count), count)
        lanes = pl.ds(pl.multiple_of(at_x * width, width), width)
        up_ref[spots, lanes] = ref[start : start + count, :].astype(f32)

    def put_down(ref, start, at_x, at_y):
        spots = pl.ds(pl.multiple_of((2 * at_y + at_x) * count, count), count)
        down_ref[spots, :] = ref[start : start + count, :].astype(f32)

    put_up(a, 0, x, y)
    put_up(a_near, 0, x, 1 - y)
    put_up(a_far, 0, 1 - x, y)
    put_up(a_far, count, 1 - x, 1 - y)
    put_down(b, 0, x, y)
    put_down(b_near, 0, 1 - x, y)
    put_down(b_far, 0, x, 1 - y)
    put_down(b_far, count, 1 - x, 1 - y)


def unpack_mlp(x, y, *pieces):
    count, width = pieces[0].shape
    shapes = [((2 * count, 2 * width), f32), ((4 * count, width), f32)]
    return call(unpack_mlp_kernel, "unpack_mlp", 2.10, UNPACK_MIB, (x, y, *pieces), shapes)


def unpack_kernel(
    x_ref, y_ref, c, c_near, c_far, d, d_near, d_far, tab,
    q_ref, k_ref, v_ref, out_ref, tab_ref, first, second,
):
    x, y = x_ref[0], y_ref[0]
    count = d.shape[0]

    def put(total, ref, start, low, high):
        spots = pl.ds(pl.multiple_of((2 * low + high) * count, count), count)
        total[spots, :] = ref[start : start + count, :].astype(f32)

    put(first, c, 0, x, y)
    put(first, c_near, 0, x, 1 - y)
    put(first, c_far, 0, 1 - x, y)
    put(first, c_far, count, 1 - x, 1 - y)
    put(second, d, 0, y, x)
    put(second, d_near, 0, y, 1 - x)
    put(second, d_far, 0, 1 - y, x)
    put(second, d_far, count, 1 - y, 1 - x)
    wide = q_ref.shape[1]
    out_rows = out_ref.shape[0]
    levels = tab_ref.shape[1]
    q_ref[...] = first[:, :wide]
    k_ref[...] = first[:, wide:]
    v_ref[...] = second[:, :wide]
    out_ref[:, :wide] = second[:out_rows, wide:]
    out_ref[:, wide:] = second[out_rows:, wide:]
    table = tab[...] + c_far[2 * count :, :].astype(f32)
    tab_ref[0] = table[:levels, :wide]
    tab_ref[1] = table[:levels, wide:]
    tab_ref[2] = table[levels:, :wide]
    tab_ref[3] = table[levels:, wide:]


def unpack(x, y, c, c_near, c_far, d, d_near, d_far, tab, wide, rows):
    count, width = d.shape
    depth = 4 * count
    shapes = [((depth, wide), f32)] * 3
    shapes += [((rows, width), f32), ((4, tab.shape[0] // 2, wide), f32)]
    scratch = [pltpu.VMEM((depth, width), f32)] * 2
    operands = (x, y, c, c_near, c_far, d, d_near, d_far, tab)
    return call(unpack_kernel, "unpack", 5.60, UNPACK_MIB, operands, shapes, scratch)


def passed_along(block, axis, distance):
    devices = range(lax.axis_size(axis))
    route = [((i - distance) % len(devices), i) for i in devices]
    return lax.ppermute(block, axis, route)


def swapped(block, axis, bit):
    devices = range(lax.axis_size(axis))
    return lax.ppermute(block, axis, [(i, i ^ bit) for i in devices])


def together(*blocks):
    return lax.optimization_barrier(blocks)


def held_until(block, *others):
    return lax.optimization_barrier((block, *others))[0]


def two_parts(block, axis, bit):
    half = block.shape[0] // 2
    upper = (lax.axis_index(axis) & bit) != 0
    send = jnp.where(upper, block[:half], block[half:])
    keep = jnp.where(upper, block[half:], block[:half])
    return send, keep


def added(keep, got):
    return (keep.astype(f32) + got.astype(f32)).astype(bf16)


def picked(pieces, place, j):
    return jnp.where(
        place == 0,
        pieces[j],
        jnp.where(
            place == 1, pieces[1 ^ j], jnp.where(place == 2, pieces[2 ^ j], pieces[3 ^ j])
        ),
    )


def quarters(block, place):
    count = block.shape[0] // 4
    pieces = [block[i * count : (i + 1) * count] for i in range(4)]
    return [picked(pieces, place, j) for j in range(4)]


def to_others(pieces, axis, bit):
    return [swapped(piece, axis, (j + 1) * bit) for j, piece in enumerate(pieces)]


def total(pieces):
    result = pieces[0].astype(f32)
    for piece in pieces[1:]:
        result = result + piece.astype(f32)
    return result


def sum_further(block, axis):
    size = lax.axis_size(axis)
    if size > 16:
        groups = [[j * 16 + i for j in range(size // 16)] for i in range(16)]
        block = lax.psum(block, axis, axis_index_groups=groups)
    return block


def body(
    inputs,
    w_query,
    w_key,
    w_value,
    w_out,
    w_up,
    w_down,
    mod_table,
    level_ids,
    neighbours,
    cotangent,
):
    rows, half = inputs.shape
    width = half * lax.axis_size("heads")
    levels = mod_table.shape[1]
    head = lax.axis_index("heads").astype(jnp.int32).reshape(1)
    first_head = lax.axis_index("heads") == 0
    ids_own = level_ids[None, :]

    before = passed_along(inputs, "nodes", 1)
    after = passed_along(inputs, "nodes", -1)
    in_other = swapped(inputs, "heads", 1)
    cot_other = swapped(cotangent, "heads", 1)
    own = front(head, ids_own, inputs, in_other, mod_table, w_key, w_value, w_query)
    queries, keys_t1, values1 = own[4:]
    ids_late = held_until(ids_own, own[0])
    ids_before = passed_along(ids_late, "nodes", 1)
    ids_after = passed_along(ids_late, "nodes", -1)
    node_count = rows * lax.axis_size("nodes")
    first_node = lax.axis_index("nodes") * rows
    places = jnp.mod(neighbours.T - first_node + SPAN, node_count)
    full_cot = jnp.where(
        first_head,
        jnp.concatenate([cotangent, cot_other], axis=1),
        jnp.concatenate([cot_other, cotangent], axis=1),
    )
    grad_act = dot(full_cot, w_down, 1, 1).astype(bf16)
    before, after = held_until((before, after), own[0], grad_act, ids_before, ids_after)
    before_other = swapped(before, "heads", 1)
    low = front(head, ids_before, before, before_other, mod_table, w_key, w_value)
    after_other = swapped(after, "heads", 1)
    high = front(head, ids_after, after, after_other, mod_table, w_key, w_value)
    normed, units, keys, values_t = zip(low, own[:4], high)
    weights, mixed_t, inverse, attn_part = attend(places, keys, values_t, queries, w_out)
    attn_other = swapped(attn_part, "heads", 1)
    middle, two_part, mlp_theirs, out_mine, normed_two, activated, grad_pre = mlp(
        head, ids_own, inputs, in_other, attn_part, attn_other, grad_act, mod_table, w_up, w_down
    )
    two_other = swapped(two_part, "heads", 1)
    grad_up = dot(normed_two, grad_pre, 0, 0).astype(bf16)
    grad_down = dot(activated, full_cot, 0, 0).astype(bf16)
    hidden = grad_up.shape[1] // 2
    grad_up = jnp.concatenate([grad_up[:, :hidden], grad_up[:, hidden:]])
    up_send, up_keep = two_parts(grad_up, "nodes", 1)
    down_send, down_keep = two_parts(grad_down, "nodes", 2)
    place = lax.axis_index("nodes").astype(jnp.int32).reshape(1)
    x, y, z_low, z_high = [jnp.bitwise_and(jnp.right_shift(place, bit), 1) for bit in range(4)]
    up_got = swapped(up_send, "nodes", 1)
    down_got = swapped(down_send, "nodes", 2)
    mlp_other = swapped(mlp_theirs, "heads", 1)
    output = (out_mine + mlp_other.astype(f32)).astype(bf16)

    keys_t = [
        dot(w_key, normed[0], 0, 1).astype(bf16),
        keys_t1,
        dot(w_key, normed[2], 0, 1).astype(bf16),
    ]
    values = [
        dot(normed[0], w_value, 1, 0).astype(bf16),
        values1,
        dot(normed[2], w_value, 1, 0).astype(bf16),
    ]
    mid_mine, grad_out, tab_two, grad_t, cross = branch(
        head, ids_own, middle, cotangent, cot_other, two_part, two_other, mixed_t, inverse,
        mod_table, w_out,
    )
    grad_t = held_until(grad_t, up_send, down_send)
    dkv, dq = backward(weights, grad_t, cross, queries, values, keys_t)
    up_send, up_keep = two_parts(added(up_keep, held_until(up_got, dq)), "nodes", 2)
    down_send, down_keep = two_parts(added(down_keep, held_until(down_got, dq)), "nodes", 1)
    up_got = swapped(up_send, "nodes", 2)
    down_got = swapped(down_send, "nodes", 1)
    dq = held_until(dq, up_send, down_send)
    grad_q, grad_kv, one_mine, one_theirs, tab_mine, tab_theirs = grads(
        head, dkv, dq, (ids_before, ids_own, ids_after), normed, units,
        w_key, w_value, w_query, levels,
    )
    one_other = swapped(one_theirs, "heads", 1)
    tab_other = swapped(tab_theirs, "heads", 1)
    up_got, down_got = held_until((up_got, down_got), grad_q)
    grad_q, grad_kv, grad_out = sum_further((grad_q, grad_kv, grad_out), "nodes")
    wide = grad_q.shape[1]
    spot = jnp.bitwise_and(jnp.right_shift(lax.axis_index("nodes"), 2), 3)
    m = jnp.concatenate([added(up_keep, up_got), added(down_keep, down_got)])
    m_parts = quarters(m, spot)
    c = jnp.concatenate([grad_q, grad_kv[:, :wide]], axis=1)
    d = jnp.concatenate([grad_out[:, :wide], grad_out[:, wide:]], axis=0)
    d = jnp.concatenate([grad_kv[:, wide:], d], axis=1)
    c_send, c_keep = two_parts(c, "nodes", 1)
    d_send, d_keep = two_parts(d, "nodes", 2)
    c_send, d_send, *m_parts = together(c_send, d_send, *m_parts)
    c_got, d_got, tab_other, one_other, *m_got = together(
        swapped(c_send, "nodes", 1),
        swapped(d_send, "nodes", 2),
        tab_other,
        one_other,
        *to_others(m_parts[1:], "nodes", 4),
    )
    c_send, c_keep = two_parts(added(c_keep, c_got), "nodes", 2)
    d_send, d_keep = two_parts(added(d_keep, d_got), "nodes", 1)
    m = sum_further(total([m_parts[0], *m_got]).astype(bf16), "nodes")
    one_all = one_mine.astype(f32) + one_other.astype(f32)
    to_before, to_after = one_all[:rows].astype(bf16), one_all[2 * rows :].astype(bf16)
    c_send, d_send, m, to_before, to_after = together(c_send, d_send, m, to_before, to_after)
    to_before = passed_along(to_before, "nodes", -1)
    to_after = passed_along(to_after, "nodes", 1)
    c_got, d_got, *m_got = together(
        swapped(c_send, "nodes", 2),
        swapped(d_send, "nodes", 1),
        *to_others([m] * 3, "nodes", 4),
    )
    m_parts = [picked([m, *m_got], spot, i) for i in range(4)]
    a, b = jnp.concatenate(m_parts[:2]), jnp.concatenate(m_parts[2:])
    table = sum_further(jnp.concatenate([tab_mine + tab_other, tab_two], axis=0), "nodes")
    cd = jnp.concatenate(
        [total([c_keep, c_got]), total([d_keep, d_got]), table], axis=0
    ).astype(bf16)
    a, b, *cd_parts = together(a, b, *quarters(cd, spot))
    cd_got = together(*to_others(cd_parts[1:], "nodes", 4))
    cd = total([cd_parts[0], *cd_got]).astype(bf16)
    a, b, cd, to_before, to_after = together(a, b, cd, to_before, to_after)
    a_near, b_near, *cd_got = together(
        swapped(a, "nodes", 2),
        swapped(b, "nodes", 1),
        *to_others([cd] * 3, "nodes", 4),
    )
    cd = jnp.concatenate([picked([cd, *cd_got], spot, i) for i in range(4)])
    count = cd.shape[0] // 2 - levels
    a_send, b_send, c, d = together(
        jnp.concatenate([a, a_near]),
        jnp.concatenate([b, b_near]),
        jnp.concatenate([cd[:count], cd[2 * count :]]),
        cd[count : 2 * count],
    )
    grad_one = one_all[rows : 2 * rows] + to_before.astype(f32) + to_after.astype(f32)
    full_in = jnp.concatenate([inputs, in_other], axis=1).astype(f32)
    unit, inverse = norm_rows(full_in)
    unit = unit[:, :half]
    onehot = (level_ids[:, None] == jnp.arange(levels, dtype=jnp.int32)[None, :]).astype(f32)
    scale_mine = jnp.where(first_head, mod_table[0][:, :half], mod_table[0][:, half:])
    gain = 1.0 + jnp.dot(onehot, scale_mine, precision=lax.Precision.HIGHEST)
    gained = grad_one * gain
    sum_gain, sum_cross = lax.psum(
        (jnp.sum(gained, axis=1), jnp.sum(gained * unit, axis=1)), "heads"
    )
    grad_inputs = mid_mine + inverse * (
        gained - sum_gain[:, None] / width - unit * sum_cross[:, None] / width
    )
    a_far, b_far, c_near, d_near, grad_inputs = together(
        swapped(a_send, "nodes", 1),
        swapped(b_send, "nodes", 2),
        swapped(c, "nodes", 2),
        swapped(d, "nodes", 1),
        grad_inputs,
    )
    tab = total([c[count:], c_near[count:]])
    c_send = jnp.concatenate([c[:count], c_near[:count], tab.astype(bf16)])
    c_far = swapped(c_send, "nodes", 1)
    d_far = swapped(jnp.concatenate([d, d_near]), "nodes", 2)
    up_total, down_total = unpack_mlp(x, y, a, a_near, a_far, b, b_near, b_far)
    c_far, d_far = held_until((c_far, d_far), up_total)
    query_total, key_total, value_total, out_total, table_total = unpack(
        x, y, c, c_near, c_far, d, d_near, d_far, tab, wide, grad_out.shape[0]
    )
    return (
        output,
        grad_inputs,
        query_total,
        key_total,
        value_total,
        out_total,
        up_total,
        down_total,
        table_total,
    )


def solution(mesh):
    return jax.shard_map(
        body,
        mesh=mesh,
        in_specs=(
            P("nodes", "heads"),
            P(None, "heads"),
            P(None, "heads"),
            P(None, "heads"),
            P("heads", None),
            P(None, "heads"),
            P("heads", None),
            P(),
            P("nodes"),
            P("nodes", None),
            P("nodes", "heads"),
        ),
        out_specs=(
            P("nodes", "heads"),
            P("nodes", "heads"),
            P(None, "heads"),
            P(None, "heads"),
            P(None, "heads"),
            P("heads", None),
            P(None, "heads"),
            P("heads", None),
            P(None, None, "heads"),
        ),
        check_vma=False,
    )
```

```python
import math

import jax
import jax.numpy as jnp
from jax import lax
from jax.experimental import pallas as pl
from jax.experimental.pallas import tpu as pltpu
from jax.sharding import PartitionSpec as P

HD = 128
K = 16
SPAN = 896
ROWS = 128
WORD = 64
HUGE = -1e30
MIB = 1024 * 1024
FRONT_MIB = 20
ATTEND_MIB = 20
MLP_MIB = 24
BRANCH_MIB = 14
BACK_MIB = 32
GRADS_MIB = 20
UNPACK_MIB = 8
epsilon = 1e-05
bf16 = jnp.bfloat16
f32 = jnp.float32


def dot(left, right, left_dim, right_dim):
    return lax.dot_general(
        left,
        right,
        (((left_dim,), (right_dim,)), ((), ())),
        preferred_element_type=f32,
    )


def two_blocks(first, second):
    zero = jnp.zeros_like(first)
    return jnp.concatenate(
        [jnp.concatenate([first, zero], 1), jnp.concatenate([zero, second], 1)], 0
    )


def ordered(head, mine, theirs):
    return jnp.where(
        head == 0,
        jnp.concatenate([mine, theirs], axis=1),
        jnp.concatenate([theirs, mine], axis=1),
    )


def parted(head, block):
    half = block.shape[1] // 2
    low, high = block[:, :half], block[:, half:]
    return jnp.where(head == 0, low, high), jnp.where(head == 0, high, low)


def onehot_t(ids, levels):
    spots = lax.broadcasted_iota(jnp.int32, (levels, ids.shape[1]), 0)
    return jnp.where(spots == ids, 1.0, 0.0).astype(bf16)


def level_values(ids, table):
    chosen = onehot_t(ids, table.shape[0])
    first = table.astype(bf16)
    rest = table - first.astype(f32)
    second = rest.astype(bf16)
    third = (rest - second.astype(f32)).astype(bf16)
    return dot(
        jnp.concatenate([chosen] * 3, axis=0),
        jnp.concatenate([first, second, third], axis=0),
        0,
        0,
    )


def norm_rows(values):
    centred = values - jnp.mean(values, axis=1, keepdims=True)
    inverse = lax.rsqrt(jnp.mean(centred * centred, axis=1, keepdims=True) + epsilon)
    return centred * inverse, inverse


def cost(microseconds):
    return pl.CostEstimate(
        flops=int(microseconds * 5e8), bytes_accessed=int(microseconds * 2.5e6), transcendentals=0
    )


def call(kernel, name, microseconds, mebibytes, operands, out_shape, scratch=()):
    spaces = [
        pltpu.SMEM if operand.shape == (1,) else pltpu.VMEM for operand in operands
    ]
    return pl.pallas_call(
        kernel,
        in_specs=[pl.BlockSpec(memory_space=space) for space in spaces],
        out_shape=[jax.ShapeDtypeStruct(shape, kind) for shape, kind in out_shape],
        scratch_shapes=list(scratch),
        compiler_params=pltpu.CompilerParams(vmem_limit_bytes=mebibytes * MIB),
        cost_estimate=cost(microseconds),
        name=name,
    )(*operands)


def front_kernel(
    head_ref, ids_ref, mine_ref, theirs_ref, table_ref, key_ref, value_ref, *refs
):
    width = 2 * mine_ref.shape[1]
    more = len(refs) > 4
    normed_ref, unit_ref, k_ref, vt_ref = refs[-4:] if not more else refs[1:5]
    values = ordered(head_ref[0], mine_ref[...], theirs_ref[...]).astype(f32)
    unit, _ = norm_rows(values)
    level = level_values(
        ids_ref[...], jnp.concatenate([table_ref[0], table_ref[1]], axis=1)
    )
    normed = (unit * (1.0 + level[:, :width]) + level[:, width:]).astype(bf16)
    normed_ref[...] = normed
    unit_ref[...] = unit.astype(bf16)
    k_ref[...] = dot(normed, key_ref[...], 1, 0).astype(bf16)
    vt_ref[...] = dot(value_ref[...], normed, 0, 1).astype(bf16)
    if more:
        query_ref, (q_ref, kt_ref, v_ref) = refs[0], refs[5:]
        q_ref[...] = dot(normed, query_ref[...], 1, 0).astype(bf16)
        kt_ref[...] = dot(key_ref[...], normed, 0, 1).astype(bf16)
        v_ref[...] = dot(normed, value_ref[...], 1, 0).astype(bf16)


def front(head, ids, mine, theirs, table, w_key, w_value, *w_query):
    rows = mine.shape[0]
    width = 2 * mine.shape[1]
    wide = 2 * HD
    down, along = ((rows, wide), bf16), ((wide, rows), bf16)
    shapes = [((rows, width), bf16)] * 2 + [down, along]
    if w_query:
        shapes += [down, along, down]
    operands = (head, ids, mine, theirs, table, w_key, w_value, *w_query)
    return call(front_kernel, "front", 10.50, FRONT_MIB, operands, shapes)


def forward_kernel(
    nbr_ref, k0, k1, k2, vt0, vt1, vt2, q_ref, out_ref,
    e_ref, mixed_ref, inv_ref, part_ref, k_all, vt_all, s_new, s_old, top_old,
):
    blocks, window, _ = e_ref.shape
    rows = k0.shape[0]
    scale = math.log2(math.e) / math.sqrt(HD)
    for i, (k, vt) in enumerate(((k0, vt0), (k1, vt1), (k2, vt2))):
        k_all[i * rows : (i + 1) * rows, :] = k[...]
        vt_all[:, i * rows : (i + 1) * rows] = vt[...]
    s_old[...] = jnp.zeros_like(s_old)
    top_old[...] = jnp.zeros_like(top_old)

    def work(step, carry):
        old_block = jnp.maximum(step - 1, 0)
        start = pl.multiple_of(jnp.minimum(step, blocks - 1) * ROWS, ROWS)
        old_start = pl.multiple_of(old_block * ROWS, ROWS)
        place = nbr_ref[:, pl.ds(start, ROWS)] - start
        bit = jnp.left_shift(1, jnp.right_shift(place, 6))
        low = jnp.bitwise_and(place, WORD - 1)
        lane_low = lax.broadcasted_iota(jnp.int32, (WORD, ROWS), 0)
        words = jnp.zeros((WORD, ROWS), jnp.int32)
        for j in range(K):
            words = words | jnp.where(lane_low == low[j : j + 1, :], bit[j : j + 1, :], 0)
        queries = q_ref[pl.ds(start, ROWS), :]
        both = two_blocks(queries[:, :HD], queries[:, HD:])
        scores = dot(k_all[pl.ds(start, window), :], both, 1, 1)
        old = top_old[:1, :]
        top = None
        weights = []
        for t in range(window // WORD):
            there = slice(t * WORD, (t + 1) * WORD)
            keep = (words & (1 << t)) != 0
            part = scores[there, :]
            part = jnp.concatenate(
                [jnp.where(keep, part[:, :ROWS], HUGE), jnp.where(keep, part[:, ROWS:], HUGE)], 1
            )
            top = part if top is None else jnp.maximum(top, part)
            s_new[there, :] = part
            weight = jnp.exp2(s_old[there, :] * scale - old)
            weights.append(weight.astype(bf16))
        weights = jnp.concatenate(weights, 0)
        inverse = 1.0 / dot(jnp.ones((16, window), bf16), weights, 1, 0)[:1, :]
        e_ref[old_block] = weights
        there = pl.ds(old_start, ROWS)
        inv_ref[0:1, there] = inverse[:, :ROWS]
        inv_ref[1:2, there] = inverse[:, ROWS:]
        mixed = dot(vt_all[:, pl.ds(old_start, window)], weights, 1, 0) * inverse
        mixed = jnp.concatenate([mixed[:HD, :ROWS], mixed[HD:, ROWS:]], axis=0)
        mixed_ref[:, there] = mixed.astype(bf16)
        part_ref[there, :] = dot(mixed.T.astype(bf16), out_ref[...], 1, 0).astype(bf16)
        s_old[...] = s_new[...]
        top_old[...] = jnp.broadcast_to(jnp.max(top, axis=0, keepdims=True) * scale, top_old.shape)
        return carry

    lax.fori_loop(0, blocks + 1, work, 0)


def attend(places, keys, values_t, queries, w_out):
    rows = queries.shape[0]
    wide = 2 * HD
    blocks = rows // ROWS
    window = ROWS + 2 * SPAN
    shapes = [
        ((blocks, window, wide), bf16),
        ((wide, rows), bf16),
        ((8, rows), f32),
        ((rows, w_out.shape[1]), bf16),
    ]
    scratch = [
        pltpu.VMEM((3 * rows, wide), bf16),
        pltpu.VMEM((wide, 3 * rows), bf16),
        pltpu.VMEM((window, wide), f32),
        pltpu.VMEM((window, wide), f32),
        pltpu.VMEM((8, wide), f32),
    ]
    operands = (places, *keys, *values_t, queries, w_out)
    return call(forward_kernel, "attend_forward", 35.00, ATTEND_MIB, operands, shapes, scratch)


def mlp_kernel(
    head_ref, ids_ref, xm_ref, xt_ref, part_ref, other_ref, grad_ref, table_ref, up_ref, down_ref,
    middle_ref, two_ref, theirs_ref, out_ref, normed_ref, act_ref, pre_ref,
):
    head = head_ref[0]
    width = 2 * xm_ref.shape[1]
    values = ordered(head, xm_ref[...], xt_ref[...]).astype(f32)
    middle = values + (part_ref[...].astype(f32) + other_ref[...].astype(f32))
    middle_ref[...] = middle
    unit, _ = norm_rows(middle)
    level = level_values(
        ids_ref[...], jnp.concatenate([table_ref[2], table_ref[3]], axis=1)
    )
    normed = (unit * (1.0 + level[:, :width]) + level[:, width:]).astype(bf16)
    normed_ref[...] = normed
    pre = dot(normed, up_ref[...], 1, 0)
    sigma = jax.nn.sigmoid(pre)
    act = (pre * sigma).astype(bf16)
    act_ref[...] = act
    grad = grad_ref[...].astype(f32)
    grad = (grad * sigma * (1.0 + pre * (1.0 - sigma))).astype(bf16)
    pre_ref[...] = grad
    two_ref[...] = dot(grad, up_ref[...], 1, 1).astype(bf16)
    mine, theirs = parted(head, dot(act, down_ref[...], 1, 0))
    theirs_ref[...] = theirs.astype(bf16)
    out_ref[...] = parted(head, middle)[0] + mine


def mlp(head, ids, x_mine, x_theirs, part, other, grad_act, table, w_up, w_down):
    rows, half = x_mine.shape
    hidden = w_up.shape[1]
    shapes = [
        (2 * half, f32), (2 * half, bf16), (half, bf16), (half, f32),
        (2 * half, bf16), (hidden, bf16), (hidden, bf16),
    ]
    shapes = [((rows, wide), kind) for wide, kind in shapes]
    operands = (head, ids, x_mine, x_theirs, part, other, grad_act, table, w_up, w_down)
    return call(mlp_kernel, "mlp", 10.50, MLP_MIB, operands, shapes)


def branch_kernel(
    head_ref, ids_ref, middle_ref, cm_ref, ct_ref, two_ref, other_ref, mixed_ref, inv_ref, table_ref, out_ref,
    mid_ref, gout_ref, tab_ref, grad_ref, cross_ref,
):
    head = head_ref[0]
    ids = ids_ref[...]
    unit, inverse = norm_rows(middle_ref[...])
    gain = 1.0 + level_values(ids, table_ref[2])
    grad_two = two_ref[...].astype(f32) + other_ref[...].astype(f32)
    gained = grad_two * gain
    cot = ordered(head, cm_ref[...], ct_ref[...]).astype(f32)
    grad_mid = cot + inverse * (
        gained
        - jnp.mean(gained, axis=1, keepdims=True)
        - unit * jnp.mean(gained * unit, axis=1, keepdims=True)
    )
    mid_ref[...] = parted(head, grad_mid)[0]
    branch = grad_mid.astype(bf16)
    grad = dot(out_ref[...], branch, 1, 1)
    cross = grad * mixed_ref[...].astype(f32)
    for h in range(grad.shape[0] // HD):
        there = slice(h * HD, (h + 1) * HD)
        total = inv_ref[h : h + 1, :]
        grad_ref[there, :] = (grad[there, :] * total).astype(bf16)
        cross_ref[h : h + 1, :] = jnp.sum(cross[there, :], axis=0, keepdims=True) * total
    gout_ref[...] = dot(mixed_ref[...], branch, 1, 0).astype(bf16)
    tab_ref[...] = dot(
        onehot_t(ids, table_ref.shape[1]),
        jnp.concatenate(
            [parted(head, grad_two * unit)[0], parted(head, grad_two)[0]], 1
        ).astype(bf16),
        1,
        0,
    )


def branch(
    head, ids, middle, cot_mine, cot_theirs, two_part, two_other, mixed_t, inverse,
    table, w_out,
):
    rows, half = cot_mine.shape
    width = 2 * half
    shapes = [
        ((rows, half), f32),
        ((w_out.shape[0], width), bf16),
        ((table.shape[1], width), f32),
        ((2 * HD, rows), bf16),
        ((8, rows), f32),
    ]
    operands = (
        head, ids, middle, cot_mine, cot_theirs, two_part, two_other, mixed_t, inverse,
        table, w_out,
    )
    return call(branch_kernel, "branch", 6.30, BRANCH_MIB, operands, shapes)


def backward_kernel(
    e_ref, grad_ref, cross_ref, q_ref, v0, v1, v2, kt0, kt1, kt2,
    dkv_ref, dq_ref, dkv_sum, kt_all, v_all, ds_slots,
):
    blocks, window, wide = e_ref.shape
    rows = v0.shape[0]
    factor = 1.0 / math.sqrt(HD)
    dkv_sum[...] = jnp.zeros_like(dkv_sum)
    for i, (v, kt) in enumerate(((v0, kt0), (v1, kt1), (v2, kt2))):
        v_all[i * rows : (i + 1) * rows, :] = v[...]
        kt_all[:, i * rows : (i + 1) * rows] = kt[...]

    def scores_and_values(block):
        start = pl.multiple_of(block * ROWS, ROWS)
        grad = grad_ref[:, pl.ds(start, ROWS)]
        grad_both = two_blocks(grad[:HD, :], grad[HD:, :])
        cross = jnp.concatenate(
            [cross_ref[0:1, pl.ds(start, ROWS)], cross_ref[1:2, pl.ds(start, ROWS)]], axis=1
        )
        weights = e_ref[block]
        spots = pl.ds(start, window)
        grad_probs = dot(v_all[spots, :], grad_both, 1, 0)
        ds_slots[block % 2] = (weights.astype(f32) * (grad_probs - cross)).astype(bf16)
        dkv_sum[spots, wide:] += dot(weights, grad_both, 1, 1)

    def keys_and_queries(block):
        start = pl.multiple_of(block * ROWS, ROWS)
        spots = pl.ds(start, window)
        queries = q_ref[pl.ds(start, ROWS), :]
        both = two_blocks(queries[:, :HD], queries[:, HD:])
        grad_scores = ds_slots[block % 2]
        dkv_sum[spots, :wide] += dot(grad_scores, both, 1, 0)
        grad_query = dot(kt_all[:, spots], grad_scores, 1, 0) * factor
        dq_ref[pl.ds(start, ROWS), :HD] = grad_query[:HD, :ROWS].T.astype(bf16)
        dq_ref[pl.ds(start, ROWS), HD:] = grad_query[HD:, ROWS:].T.astype(bf16)

    def work(block, carry):
        scores_and_values(block)
        keys_and_queries(block - 1)
        return carry

    scores_and_values(0)
    lax.fori_loop(1, blocks, work, 0)
    keys_and_queries(blocks - 1)
    for i in range(3):
        there = slice(i * rows, (i + 1) * rows)
        dkv_ref[there, :wide] = (dkv_sum[there, :wide] * factor).astype(bf16)
        dkv_ref[there, wide:] = dkv_sum[there, wide:].astype(bf16)


def backward(weights, grad_t, cross, queries, values, keys_t):
    rows = queries.shape[0]
    wide = 2 * HD
    window = weights.shape[1]
    shapes = [((3 * rows, 2 * wide), bf16), ((rows, wide), bf16)]
    scratch = [
        pltpu.VMEM((3 * rows, 2 * wide), f32),
        pltpu.VMEM((wide, 3 * rows), bf16),
        pltpu.VMEM((3 * rows, wide), bf16),
        pltpu.VMEM((2, window, wide), bf16),
    ]
    operands = (weights, grad_t, cross, queries, *values, *keys_t)
    return call(backward_kernel, "attend_backward", 67.20, BACK_MIB, operands, shapes, scratch)


def grads_kernel(
    head_ref, dkv_ref, dq_ref, id0, id1, id2, n0, n1, n2, u0, u1, u2, key_ref, value_ref, query_ref,
    gq_ref, gkv_ref, mine_ref, theirs_ref, tab_mine, tab_theirs,
):
    head = head_ref[0]
    rows, width = n0.shape
    wide = dq_ref.shape[1]
    levels = tab_mine.shape[0]
    w_kv = jnp.concatenate([key_ref[...], value_ref[...]], axis=1)
    grad_kv = jnp.zeros((width, 2 * wide), f32)
    table_sum = jnp.zeros((levels, 2 * width), f32)
    for i, (ids, normed, units) in enumerate(((id0, n0, u0), (id1, n1, u1), (id2, n2, u2))):
        there = slice(i * rows, (i + 1) * rows)
        dkv = dkv_ref[there, :]
        grad_kv = grad_kv + dot(normed[...], dkv, 0, 0)
        part = dot(dkv, w_kv, 1, 1)
        if i == 1:
            part = part + dot(dq_ref[...], query_ref[...], 1, 1)
        mine, theirs = parted(head, part)
        mine_ref[there, :] = mine.astype(bf16)
        theirs_ref[there, :] = theirs.astype(bf16)
        table_sum = table_sum + dot(
            onehot_t(ids[...], levels),
            jnp.concatenate([part * units[...].astype(f32), part], 1).astype(bf16),
            1,
            0,
        )
    gkv_ref[...] = grad_kv.astype(bf16)
    gq_ref[...] = dot(n1[...], dq_ref[...], 0, 0).astype(bf16)
    scale_mine, scale_theirs = parted(head, table_sum[:, :width])
    shift_mine, shift_theirs = parted(head, table_sum[:, width:])
    tab_mine[...] = jnp.concatenate([scale_mine, shift_mine], axis=1)
    tab_theirs[...] = jnp.concatenate([scale_theirs, shift_theirs], axis=1)


def grads(head, dkv, dq, ids, normed, units, w_key, w_value, w_query, levels):
    rows, width = normed[0].shape
    half = width // 2
    wide = dq.shape[1]
    shapes = [
        ((width, wide), bf16),
        ((width, 2 * wide), bf16),
        ((3 * rows, half), bf16),
        ((3 * rows, half), bf16),
        ((levels, width), f32),
        ((levels, width), f32),
    ]
    operands = (head, dkv, dq, *ids, *normed, *units, w_key, w_value, w_query)
    return call(grads_kernel, "grads", 17.50, GRADS_MIB, operands, shapes)


def unpack_mlp_kernel(x_ref, y_ref, a, a_near, a_far, b, b_near, b_far, up_ref, down_ref):
    x, y = x_ref[0], y_ref[0]
    count, width = a.shape

    def put_up(ref, start, at_x, at_y):
        spots = pl.ds(pl.multiple_of(at_y * count, count), count)
        lanes = pl.ds(pl.multiple_of(at_x * width, width), width)
        up_ref[spots, lanes] = ref[start : start + count, :].astype(f32)

    def put_down(ref, start, at_x, at_y):
        spots = pl.ds(pl.multiple_of((2 * at_y + at_x) * count, count), count)
        down_ref[spots, :] = ref[start : start + count, :].astype(f32)

    put_up(a, 0, x, y)
    put_up(a_near, 0, x, 1 - y)
    put_up(a_far, 0, 1 - x, y)
    put_up(a_far, count, 1 - x, 1 - y)
    put_down(b, 0, x, y)
    put_down(b_near, 0, 1 - x, y)
    put_down(b_far, 0, x, 1 - y)
    put_down(b_far, count, 1 - x, 1 - y)


def unpack_mlp(x, y, *pieces):
    count, width = pieces[0].shape
    shapes = [((2 * count, 2 * width), f32), ((4 * count, width), f32)]
    return call(unpack_mlp_kernel, "unpack_mlp", 2.10, UNPACK_MIB, (x, y, *pieces), shapes)


def unpack_kernel(
    x_ref, y_ref, c, c_near, c_far, d, d_near, d_far, tab,
    q_ref, k_ref, v_ref, out_ref, tab_ref, first, second,
):
    x, y = x_ref[0], y_ref[0]
    count = d.shape[0]

    def put(total, ref, start, low, high):
        spots = pl.ds(pl.multiple_of((2 * low + high) * count, count), count)
        total[spots, :] = ref[start : start + count, :].astype(f32)

    put(first, c, 0, x, y)
    put(first, c_near, 0, x, 1 - y)
    put(first, c_far, 0, 1 - x, y)
    put(first, c_far, count, 1 - x, 1 - y)
    put(second, d, 0, y, x)
    put(second, d_near, 0, y, 1 - x)
    put(second, d_far, 0, 1 - y, x)
    put(second, d_far, count, 1 - y, 1 - x)
    wide = q_ref.shape[1]
    out_rows = out_ref.shape[0]
    levels = tab_ref.shape[1]
    q_ref[...] = first[:, :wide]
    k_ref[...] = first[:, wide:]
    v_ref[...] = second[:, :wide]
    out_ref[:, :wide] = second[:out_rows, wide:]
    out_ref[:, wide:] = second[out_rows:, wide:]
    table = tab[...] + c_far[2 * count :, :].astype(f32)
    tab_ref[0] = table[:levels, :wide]
    tab_ref[1] = table[:levels, wide:]
    tab_ref[2] = table[levels:, :wide]
    tab_ref[3] = table[levels:, wide:]


def unpack(x, y, c, c_near, c_far, d, d_near, d_far, tab, wide, rows):
    count, width = d.shape
    depth = 4 * count
    shapes = [((depth, wide), f32)] * 3
    shapes += [((rows, width), f32), ((4, tab.shape[0] // 2, wide), f32)]
    scratch = [pltpu.VMEM((depth, width), f32)] * 2
    operands = (x, y, c, c_near, c_far, d, d_near, d_far, tab)
    return call(unpack_kernel, "unpack", 5.60, UNPACK_MIB, operands, shapes, scratch)


def passed_along(block, axis, distance):
    devices = range(lax.axis_size(axis))
    route = [((i - distance) % len(devices), i) for i in devices]
    return lax.ppermute(block, axis, route)


def swapped(block, axis, bit):
    devices = range(lax.axis_size(axis))
    return lax.ppermute(block, axis, [(i, i ^ bit) for i in devices])


def together(*blocks):
    return lax.optimization_barrier(blocks)


def held_until(block, *others):
    return lax.optimization_barrier((block, *others))[0]


def two_parts(block, axis, bit):
    half = block.shape[0] // 2
    upper = (lax.axis_index(axis) & bit) != 0
    send = jnp.where(upper, block[:half], block[half:])
    keep = jnp.where(upper, block[half:], block[:half])
    return send, keep


def added(keep, got):
    return (keep.astype(f32) + got.astype(f32)).astype(bf16)


def picked(pieces, place, j):
    return jnp.where(
        place == 0,
        pieces[j],
        jnp.where(
            place == 1, pieces[1 ^ j], jnp.where(place == 2, pieces[2 ^ j], pieces[3 ^ j])
        ),
    )


def quarters(block, place):
    count = block.shape[0] // 4
    pieces = [block[i * count : (i + 1) * count] for i in range(4)]
    return [picked(pieces, place, j) for j in range(4)]


def to_others(pieces, axis, bit):
    return [swapped(piece, axis, (j + 1) * bit) for j, piece in enumerate(pieces)]


def total(pieces):
    result = pieces[0].astype(f32)
    for piece in pieces[1:]:
        result = result + piece.astype(f32)
    return result


def sum_further(block, axis):
    size = lax.axis_size(axis)
    if size > 16:
        groups = [[j * 16 + i for j in range(size // 16)] for i in range(16)]
        block = lax.psum(block, axis, axis_index_groups=groups)
    return block


def body(
    inputs,
    w_query,
    w_key,
    w_value,
    w_out,
    w_up,
    w_down,
    mod_table,
    level_ids,
    neighbours,
    cotangent,
):
    rows, half = inputs.shape
    width = half * lax.axis_size("heads")
    levels = mod_table.shape[1]
    head = lax.axis_index("heads").astype(jnp.int32).reshape(1)
    first_head = lax.axis_index("heads") == 0
    ids_own = level_ids[None, :]

    before = passed_along(inputs, "nodes", 1)
    after = passed_along(inputs, "nodes", -1)
    in_other = swapped(inputs, "heads", 1)
    cot_other = swapped(cotangent, "heads", 1)
    own = front(head, ids_own, inputs, in_other, mod_table, w_key, w_value, w_query)
    queries, keys_t1, values1 = own[4:]
    ids_late = held_until(ids_own, own[0])
    ids_before = passed_along(ids_late, "nodes", 1)
    ids_after = passed_along(ids_late, "nodes", -1)
    node_count = rows * lax.axis_size("nodes")
    first_node = lax.axis_index("nodes") * rows
    places = jnp.mod(neighbours.T - first_node + SPAN, node_count)
    full_cot = jnp.where(
        first_head,
        jnp.concatenate([cotangent, cot_other], axis=1),
        jnp.concatenate([cot_other, cotangent], axis=1),
    )
    grad_act = dot(full_cot, w_down, 1, 1).astype(bf16)
    before, after = held_until((before, after), own[0], grad_act, ids_before, ids_after)
    before_other = swapped(before, "heads", 1)
    low = front(head, ids_before, before, before_other, mod_table, w_key, w_value)
    after_other = swapped(after, "heads", 1)
    high = front(head, ids_after, after, after_other, mod_table, w_key, w_value)
    normed, units, keys, values_t = zip(low, own[:4], high)
    weights, mixed_t, inverse, attn_part = attend(places, keys, values_t, queries, w_out)
    attn_other = swapped(attn_part, "heads", 1)
    middle, two_part, mlp_theirs, out_mine, normed_two, activated, grad_pre = mlp(
        head, ids_own, inputs, in_other, attn_part, attn_other, grad_act, mod_table, w_up, w_down
    )
    two_other = swapped(two_part, "heads", 1)
    grad_up = dot(normed_two, grad_pre, 0, 0).astype(bf16)
    grad_down = dot(activated, full_cot, 0, 0).astype(bf16)
    hidden = grad_up.shape[1] // 2
    grad_up = jnp.concatenate([grad_up[:, :hidden], grad_up[:, hidden:]])
    up_send, up_keep = two_parts(grad_up, "nodes", 1)
    down_send, down_keep = two_parts(grad_down, "nodes", 2)
    place = lax.axis_index("nodes").astype(jnp.int32).reshape(1)
    x, y, z_low, z_high = [jnp.bitwise_and(jnp.right_shift(place, bit), 1) for bit in range(4)]
    up_got = swapped(up_send, "nodes", 1)
    down_got = swapped(down_send, "nodes", 2)
    mlp_other = swapped(mlp_theirs, "heads", 1)
    output = (out_mine + mlp_other.astype(f32)).astype(bf16)

    keys_t = [
        dot(w_key, normed[0], 0, 1).astype(bf16),
        keys_t1,
        dot(w_key, normed[2], 0, 1).astype(bf16),
    ]
    values = [
        dot(normed[0], w_value, 1, 0).astype(bf16),
        values1,
        dot(normed[2], w_value, 1, 0).astype(bf16),
    ]
    mid_mine, grad_out, tab_two, grad_t, cross = branch(
        head, ids_own, middle, cotangent, cot_other, two_part, two_other, mixed_t, inverse,
        mod_table, w_out,
    )
    grad_t = held_until(grad_t, up_send, down_send)
    dkv, dq = backward(weights, grad_t, cross, queries, values, keys_t)
    up_send, up_keep = two_parts(added(up_keep, held_until(up_got, dq)), "nodes", 2)
    down_send, down_keep = two_parts(added(down_keep, held_until(down_got, dq)), "nodes", 1)
    up_got = swapped(up_send, "nodes", 2)
    down_got = swapped(down_send, "nodes", 1)
    dq = held_until(dq, up_send, down_send)
    grad_q, grad_kv, one_mine, one_theirs, tab_mine, tab_theirs = grads(
        head, dkv, dq, (ids_before, ids_own, ids_after), normed, units,
        w_key, w_value, w_query, levels,
    )
    one_other = swapped(one_theirs, "heads", 1)
    tab_other = swapped(tab_theirs, "heads", 1)
    up_got, down_got = held_until((up_got, down_got), grad_q)
    grad_q, grad_kv, grad_out = sum_further((grad_q, grad_kv, grad_out), "nodes")
    wide = grad_q.shape[1]
    spot = jnp.bitwise_and(jnp.right_shift(lax.axis_index("nodes"), 2), 3)
    m = jnp.concatenate([added(up_keep, up_got), added(down_keep, down_got)])
    m_parts = quarters(m, spot)
    c = jnp.concatenate([grad_q, grad_kv[:, :wide]], axis=1)
    d = jnp.concatenate([grad_out[:, :wide], grad_out[:, wide:]], axis=0)
    d = jnp.concatenate([grad_kv[:, wide:], d], axis=1)
    c_send, c_keep = two_parts(c, "nodes", 1)
    d_send, d_keep = two_parts(d, "nodes", 2)
    c_send, d_send, *m_parts = together(c_send, d_send, *m_parts)
    c_got, d_got, tab_other, one_other, *m_got = together(
        swapped(c_send, "nodes", 1),
        swapped(d_send, "nodes", 2),
        tab_other,
        one_other,
        *to_others(m_parts[1:], "nodes", 4),
    )
    c_send, c_keep = two_parts(added(c_keep, c_got), "nodes", 2)
    d_send, d_keep = two_parts(added(d_keep, d_got), "nodes", 1)
    m = sum_further(total([m_parts[0], *m_got]).astype(bf16), "nodes")
    one_all = one_mine.astype(f32) + one_other.astype(f32)
    to_before, to_after = one_all[:rows].astype(bf16), one_all[2 * rows :].astype(bf16)
    c_send, d_send, m, to_before, to_after = together(c_send, d_send, m, to_before, to_after)
    to_before = passed_along(to_before, "nodes", -1)
    to_after = passed_along(to_after, "nodes", 1)
    c_got, d_got, *m_got = together(
        swapped(c_send, "nodes", 2),
        swapped(d_send, "nodes", 1),
        *to_others([m] * 3, "nodes", 4),
    )
    m_parts = [picked([m, *m_got], spot, i) for i in range(4)]
    a, b = jnp.concatenate(m_parts[:2]), jnp.concatenate(m_parts[2:])
    table = sum_further(jnp.concatenate([tab_mine + tab_other, tab_two], axis=0), "nodes")
    cd = jnp.concatenate(
        [total([c_keep, c_got]), total([d_keep, d_got]), table], axis=0
    ).astype(bf16)
    a, b, *cd_parts = together(a, b, *quarters(cd, spot))
    cd_got = together(*to_others(cd_parts[1:], "nodes", 4))
    cd = total([cd_parts[0], *cd_got]).astype(bf16)
    a, b, cd, to_before, to_after = together(a, b, cd, to_before, to_after)
    a_near, b_near, *cd_got = together(
        swapped(a, "nodes", 2),
        swapped(b, "nodes", 1),
        *to_others([cd] * 3, "nodes", 4),
    )
    cd = jnp.concatenate([picked([cd, *cd_got], spot, i) for i in range(4)])
    count = cd.shape[0] // 2 - levels
    a_send, b_send, c, d = together(
        jnp.concatenate([a, a_near]),
        jnp.concatenate([b, b_near]),
        jnp.concatenate([cd[:count], cd[2 * count :]]),
        cd[count : 2 * count],
    )
    grad_one = one_all[rows : 2 * rows] + to_before.astype(f32) + to_after.astype(f32)
    full_in = jnp.concatenate([inputs, in_other], axis=1).astype(f32)
    unit, inverse = norm_rows(full_in)
    unit = unit[:, :half]
    onehot = (level_ids[:, None] == jnp.arange(levels, dtype=jnp.int32)[None, :]).astype(f32)
    scale_mine = jnp.where(first_head, mod_table[0][:, :half], mod_table[0][:, half:])
    gain = 1.0 + jnp.dot(onehot, scale_mine, precision=lax.Precision.HIGHEST)
    gained = grad_one * gain
    sum_gain, sum_cross = lax.psum(
        (jnp.sum(gained, axis=1), jnp.sum(gained * unit, axis=1)), "heads"
    )
    grad_inputs = mid_mine + inverse * (
        gained - sum_gain[:, None] / width - unit * sum_cross[:, None] / width
    )
    a_far, b_far, c_near, d_near, grad_inputs = together(
        swapped(a_send, "nodes", 1),
        swapped(b_send, "nodes", 2),
        swapped(c, "nodes", 2),
        swapped(d, "nodes", 1),
        grad_inputs,
    )
    tab = total([c[count:], c_near[count:]])
    c_send = jnp.concatenate([c[:count], c_near[:count], tab.astype(bf16)])
    c_far = swapped(c_send, "nodes", 1)
    d_far = swapped(jnp.concatenate([d, d_near]), "nodes", 2)
    up_total, down_total = unpack_mlp(x, y, a, a_near, a_far, b, b_near, b_far)
    c_far, d_far = held_until((c_far, d_far), up_total)
    query_total, key_total, value_total, out_total, table_total = unpack(
        x, y, c, c_near, c_far, d, d_near, d_far, tab, wide, grad_out.shape[0]
    )
    return (
        output,
        grad_inputs,
        query_total,
        key_total,
        value_total,
        out_total,
        up_total,
        down_total,
        table_total,
    )


def solution(mesh):
    return jax.shard_map(
        body,
        mesh=mesh,
        in_specs=(
            P("nodes", "heads"),
            P(None, "heads"),
            P(None, "heads"),
            P(None, "heads"),
            P("heads", None),
            P(None, "heads"),
            P("heads", None),
            P(),
            P("nodes"),
            P("nodes", None),
            P("nodes", "heads"),
        ),
        out_specs=(
            P("nodes", "heads"),
            P("nodes", "heads"),
            P(None, "heads"),
            P(None, "heads"),
            P(None, "heads"),
            P("heads", None),
            P(None, "heads"),
            P("heads", None),
            P(None, None, "heads"),
        ),
        check_vma=False,
    )
```
